1024 devices in a mesh: expert: 64 (over z, y), dp: 16 (over x, core).
Axes of the slice: x: 8, y: 8, z: 8, core: 2. Of those that a mesh axis runs over, the one named last changes fastest.
Arguments:
- tokens: bfloat16 [131072, 3584], P(('expert', 'dp')), may hold values from -6 to 6
- cotangent: bfloat16 [131072, 3584], P(('expert', 'dp')), may hold values from -6 to 6
- gates: bfloat16 [131072, 2], P(('expert', 'dp')), may hold values from 0.099609375 to 1
- route_ids: int32 [131072, 2], P(('expert', 'dp')), may hold values from 0 to 127, as said below
- w_gate: bfloat16 [9728, 3584], P('expert'), may hold values from -0.09375 to 0.09375
- w_up: bfloat16 [9728, 3584], P('expert'), may hold values from -0.09375 to 0.09375
- w_down: bfloat16 [9728, 3584], P('expert'), may hold values from -0.125 to 0.125
Outputs:
- grad_tokens: bfloat16 [131072, 3584], P(('expert', 'dp'))
- grad_gate: bfloat16 [9728, 3584], P('expert', 'dp')
- grad_up: bfloat16 [9728, 3584], P('expert', 'dp')
- grad_down: bfloat16 [9728, 3584], P('expert', 'dp')
The draws below stay inside these ranges and needn't reach their ends.
Inputs may be any that keep to these rules, and one draw needn't show every extreme that they name: `route_ids`: each row names two different experts. In every aligned block of 128 rows one expert under 4 is named at least 2 times.
All inputs are finite; a program needn't handle non-finite values.
Results may differ from the reference program's by a relative error of at most 0.023.
Values may be sent and summed in bfloat16 or wider, within the bound.
No kernel may reach another device: no remote copies, remote signals or barrier semaphores. Data moves between devices by JAX's collectives and lax.ppermute only.
A program may use at most 32 MiB of HBM per device.

```python
import jax
import jax.numpy as jnp
import numpy as np
from jax import lax

D = 3584
HID = 2432
NALL = 128
EXPERTS = 4
CAP = 2
TOK_DEV = 128
SPLIT = 16
H_DEV = 152
TOKENS = 131072
N_EXPERT = 64
N_DP = 16


def draw_route_ids(key, part):
    key = jax.random.fold_in(key, 7)
    rank_key, pick_key, offset_key, hot_key, force_key, swap_key = jax.random.split(key, 6)
    blocks = TOKENS // TOK_DEV
    ranked = np.floor(4096.0 / (np.arange(NALL) + 1.0)).astype(np.int32) + 1
    shuffled = jax.random.permutation(rank_key, NALL)
    weights = jnp.asarray(ranked, jnp.int32)[shuffled]
    cumulative = jnp.cumsum(weights).astype(jnp.int32)
    pick_values = jax.random.randint(pick_key, (TOKENS,), 0, cumulative[-1], dtype=jnp.int32)
    first_route = jnp.sum((pick_values[:, None] >= cumulative[None, :]).astype(jnp.int32), axis=1)
    hot_expert = jax.random.randint(hot_key, (), 0, EXPERTS, dtype=jnp.int32)

    def forced_block(block_key):
        ordering = jax.random.permutation(block_key, TOK_DEV)
        return (ordering < CAP).astype(jnp.int32)
    forced = jax.vmap(forced_block)(jax.random.split(force_key, blocks)).reshape(TOKENS)
    first_route = jnp.where(forced == 1, hot_expert, first_route)
    offset = jax.random.randint(offset_key, (TOKENS,), 1, NALL, dtype=jnp.int32)
    second_route = (first_route + offset) % NALL
    swapped = jax.random.randint(swap_key, (TOKENS,), 0, 2, dtype=jnp.int32)
    column_one = jnp.where(swapped == 1, second_route, first_route)
    column_two = jnp.where(swapped == 1, first_route, second_route)
    return jnp.stack([column_one, column_two], axis=1).astype(jnp.int32)


def levels(own_key, dims, cuts, low, largest):
    loudness, own = 1.0, jax.random.fold_in(own_key, 6)
    for dim, shards_of in cuts:
        draws = jnp.exp(jax.random.uniform(jax.random.fold_in(own, dim), (shards_of,), jnp.float32, low / len(cuts), largest / len(cuts)))
        loudness = loudness * jnp.repeat(draws, dims[dim] // shards_of).reshape([-1 if axis == dim else 1 for axis in range(len(dims))])
    return loudness


def noise(own_key, dims, deviation, reach, cuts=(), kind=jnp.bfloat16):
    result = jax.random.normal(own_key, dims, jnp.float32) * deviation
    if len(cuts) > 0:
        result = levels(own_key, dims, cuts, -0.22, 0.18) * result
    return jnp.clip(result, min=-reach, max=reach).astype(kind)


def setup_inputs(seed: int = 0) -> dict:
    key_of = jax.random.split(jax.random.key(seed), 8)
    tokens = noise(key_of[0], (TOKENS, D), 1.0, 6.0, ((0, 1024),))
    cotangent = noise(key_of[1], (TOKENS, D), 1.0, 6.0, ((0, 1024),))
    gates = jnp.clip(0.099609375 + 0.9003906 * jax.random.uniform(key_of[2], (TOKENS, 2), jnp.float32) ** levels(key_of[2], (TOKENS, 2), ((0, 1024),), -0.2, 0.2), 0.099609375, 1.0).astype(jnp.bfloat16)
    route_ids = draw_route_ids(jax.random.fold_in(key_of[7], 71), 0)
    w_gate = noise(key_of[4], (EXPERTS * HID, D), D ** -0.5, 0.09375, ((0, 64),))
    w_up = noise(key_of[5], (EXPERTS * HID, D), D ** -0.5, 0.09375, ((0, 64),))
    w_down = noise(key_of[6], (EXPERTS * HID, D), HID ** -0.5, 0.125, ((0, 64),))
    return dict(tokens=tokens, cotangent=cotangent, gates=gates, route_ids=route_ids, w_gate=w_gate, w_up=w_up, w_down=w_down)


def route_table(route_block, expert_count, capacity):
    flat_ids = route_block.reshape(-1)
    onehot = (flat_ids[:, None] == jnp.arange(expert_count, dtype=jnp.int32)[None, :]).astype(jnp.int32)
    position = jnp.cumsum(onehot, axis=0) - 1
    slot_index = jnp.sum(onehot * position, axis=1)
    kept = (flat_ids < expert_count) & (slot_index < capacity)
    target = jnp.where(kept, flat_ids * capacity + slot_index, -1)
    slot_range = jnp.arange(expert_count * capacity, dtype=jnp.int32)
    route_grid = (target[None, :] == slot_range[:, None]).astype(jnp.float32)
    return route_grid.reshape(expert_count * capacity, route_block.shape[0], 2)


def dispatch_block(token_rows, cotan_rows, gate_pair, route_block):
    route_grid = route_table(route_block, EXPERTS, CAP)
    per_token = jnp.sum(route_grid, axis=2).astype(jnp.bfloat16)
    inputs_in = jnp.dot(per_token, token_rows, preferred_element_type=jnp.float32).astype(jnp.bfloat16)
    cotan_in = jnp.dot(per_token, cotan_rows, preferred_element_type=jnp.float32).astype(jnp.bfloat16)
    gate_in = jnp.sum(route_grid * gate_pair.astype(jnp.float32)[None], axis=(1, 2)).astype(jnp.bfloat16)
    return inputs_in, cotan_in, gate_in, per_token


def expert_work(inputs_rows, cotan_rows, gate_rows, weight_gate, weight_up, weight_down):
    gate_pre = jnp.dot(inputs_rows, weight_gate.T, preferred_element_type=jnp.float32)
    up_pre = jnp.dot(inputs_rows, weight_up.T, preferred_element_type=jnp.float32)
    sigmoid_gate = jax.nn.sigmoid(gate_pre)
    activation = gate_pre * sigmoid_gate * up_pre
    back_proj = jnp.dot(cotan_rows, weight_down.T, preferred_element_type=jnp.float32)
    gate_col = gate_rows.astype(jnp.float32)[:, None]
    grad_hidden = gate_col * back_proj
    grad_up_pre = (grad_hidden * gate_pre * sigmoid_gate).astype(jnp.bfloat16)
    grad_gate_pre = (grad_hidden * up_pre * sigmoid_gate * (1.0 + gate_pre * (1.0 - sigmoid_gate))).astype(jnp.bfloat16)
    scaled_act = (gate_col * activation).astype(jnp.bfloat16)
    grad_down = jnp.dot(scaled_act.T, cotan_rows, preferred_element_type=jnp.float32).astype(jnp.bfloat16)
    grad_gate = jnp.dot(grad_gate_pre.T, inputs_rows, preferred_element_type=jnp.float32).astype(jnp.bfloat16)
    grad_up = jnp.dot(grad_up_pre.T, inputs_rows, preferred_element_type=jnp.float32).astype(jnp.bfloat16)
    row_count = inputs_rows.shape[0]
    gate_split = grad_gate_pre.astype(jnp.float32).reshape(row_count, SPLIT, H_DEV)
    up_split = grad_up_pre.astype(jnp.float32).reshape(row_count, SPLIT, H_DEV)
    weight_gate_split = weight_gate.astype(jnp.float32).reshape(SPLIT, H_DEV, D)
    weight_up_split = weight_up.astype(jnp.float32).reshape(SPLIT, H_DEV, D)
    pieces = jnp.einsum("rgh,ghd->grd", gate_split, weight_gate_split, precision=lax.Precision.HIGHEST)
    pieces = pieces + jnp.einsum("rgh,ghd->grd", up_split, weight_up_split, precision=lax.Precision.HIGHEST)
    return grad_gate, grad_up, grad_down, pieces.astype(jnp.bfloat16)


def combine_block(pair_rows, piece_rows):
    pair_table = jnp.broadcast_to(pair_rows.reshape(EXPERTS, 1, CAP, TOK_DEV), (EXPERTS, SPLIT, CAP, TOK_DEV)).astype(jnp.float32)
    total = jnp.einsum("egpt,egpd->td", pair_table, piece_rows.astype(jnp.float32), precision=lax.Precision.HIGHEST)
    return total.astype(jnp.bfloat16)


def reference(tokens, cotangent, gates, route_ids, w_gate, w_up, w_down):
    def replica_view(array):
        shaped = array.reshape((N_EXPERT, N_DP, TOK_DEV) + array.shape[1:])
        return jnp.swapaxes(shaped, 0, 1)

    full_gate = w_gate.reshape(EXPERTS, HID, D)
    full_up = w_up.reshape(EXPERTS, HID, D)
    full_down = w_down.reshape(EXPERTS, HID, D)

    def replica_step(running, replica_items):
        token_rows, cotan_rows, gate_pairs, route_blocks = replica_items
        inputs_in, cotan_in, gate_in, per_token = jax.vmap(dispatch_block)(token_rows, cotan_rows, gate_pairs, route_blocks)
        inputs_in = inputs_in.reshape(N_EXPERT, EXPERTS, CAP, D).transpose(1, 0, 2, 3).reshape(EXPERTS, N_EXPERT * CAP, D)
        cotan_in = cotan_in.reshape(N_EXPERT, EXPERTS, CAP, D).transpose(1, 0, 2, 3).reshape(EXPERTS, N_EXPERT * CAP, D)
        gate_in = gate_in.reshape(N_EXPERT, EXPERTS, CAP).transpose(1, 0, 2).reshape(EXPERTS, N_EXPERT * CAP)
        gate_list, up_list, down_list, piece_list = [], [], [], []
        for expert in range(EXPERTS):
            grad_gate, grad_up, grad_down, pieces = expert_work(inputs_in[expert], cotan_in[expert], gate_in[expert], full_gate[expert], full_up[expert], full_down[expert])
            gate_list.append(grad_gate)
            up_list.append(grad_up)
            down_list.append(grad_down)
            piece_list.append(pieces)
        sum_gate = running[0] + jnp.stack(gate_list, axis=0).astype(jnp.float32)
        sum_up = running[1] + jnp.stack(up_list, axis=0).astype(jnp.float32)
        sum_down = running[2] + jnp.stack(down_list, axis=0).astype(jnp.float32)
        piece_rows = jnp.stack(piece_list, axis=0).reshape(EXPERTS, SPLIT, N_EXPERT, CAP, D).transpose(2, 0, 1, 3, 4)
        grad_rows = jax.vmap(combine_block)(per_token, piece_rows)
        return (sum_gate, sum_up, sum_down), grad_rows

    zeros = jnp.zeros((EXPERTS, HID, D), jnp.float32)
    replica_items = (replica_view(tokens), replica_view(cotangent), replica_view(gates), replica_view(route_ids))
    sums, grad_rows = lax.scan(replica_step, (zeros, zeros, zeros), replica_items)
    grad_tokens = jnp.swapaxes(grad_rows, 0, 1).reshape(TOKENS, D)
    grad_gate = sums[0].astype(jnp.bfloat16).reshape(EXPERTS * HID, D)
    grad_up = sums[1].astype(jnp.bfloat16).reshape(EXPERTS * HID, D)
    grad_down = sums[2].astype(jnp.bfloat16).reshape(EXPERTS * HID, D)
    return grad_tokens, grad_gate, grad_up, grad_down
```

```python
import functools

import jax
import jax.numpy as jnp
from jax import lax
from jax.experimental import pallas as pl
from jax.experimental.pallas import tpu as pltpu
from jax.sharding import PartitionSpec as P

EXPERTS = 4
CAP = 2


def select_kernel(ids_ref, gates_ref, tokens_ref, cotan_ref, send_ref, table_ref, rows_ref, sems):
    slots, tokens = table_ref.shape
    features = tokens_ref.shape[1]
    slot = lax.broadcasted_iota(jnp.int32, (slots, tokens), 0)
    expert, place = slot // CAP, slot % CAP
    first = ids_ref[0:1, :] == expert
    second = ids_ref[1:2, :] == expert
    named = jnp.where(first | second, 1.0, 0.0)
    earlier = lax.broadcasted_iota(jnp.int32, (tokens, tokens), 0) < lax.broadcasted_iota(
        jnp.int32, (tokens, tokens), 1
    )
    before = jnp.dot(
        named.astype(jnp.bfloat16),
        jnp.where(earlier, 1.0, 0.0).astype(jnp.bfloat16),
        preferred_element_type=jnp.float32,
    )
    table = jnp.where(before == place.astype(jnp.float32), named, 0.0)
    gates = gates_ref[...].astype(jnp.float32)
    gate = jnp.where(first, gates[0:1, :], gates[1:2, :])
    table_ref[...] = table.astype(jnp.bfloat16)
    for weight, source_ref, start in (
        (table, tokens_ref, 0),
        (table * gate, cotan_ref, features),
    ):
        picked = jnp.dot(
            weight.astype(jnp.bfloat16), source_ref[...], preferred_element_type=jnp.float32
        )
        for e in range(EXPERTS):
            rows_ref[e, :, start : start + features] = picked[e * CAP : (e + 1) * CAP].astype(
                jnp.bfloat16
            )
    copies = [
        pltpu.make_async_copy(rows_ref, send_ref.at[:, piece], sems.at[piece])
        for piece in range(send_ref.shape[1])
    ]
    for copy in copies:
        copy.start()
    for copy in copies:
        copy.wait()


def grads_kernel(width, core_ref, rows_ref, gate_ref, up_ref, down_ref, mine_ref, other_ref, pre_ref):
    sources, cap, both = rows_ref.shape
    features = both // 2
    chunks, _, lanes = mine_ref.shape
    inputs = rows_ref[:, :, :features].reshape(sources * cap, features)
    cotan = rows_ref[:, :, features:].reshape(sources * cap, features)
    across = (((1,), (1,)), ((), ()))
    gate_pre = lax.dot_general(gate_ref[...], inputs, across, preferred_element_type=jnp.float32)
    up_pre = lax.dot_general(up_ref[...], inputs, across, preferred_element_type=jnp.float32)
    hidden = lax.dot_general(down_ref[...], cotan, across, preferred_element_type=jnp.float32)
    sig = 1.0 / (1.0 + jnp.exp(-gate_pre))
    activation = (gate_pre * sig * up_pre).astype(jnp.bfloat16)
    grad_up = hidden * gate_pre * sig
    grad_gate = hidden * up_pre * sig * (1.0 + gate_pre * (1.0 - sig))
    pre = jnp.concatenate([grad_gate, grad_up], axis=0).astype(jnp.bfloat16)
    pre_ref[...] = pre
    beyond = jnp.zeros((sources * cap, lanes - lanes // 2), jnp.bfloat16)
    inputs = jnp.concatenate([inputs, beyond], axis=1)
    cotan = jnp.concatenate([cotan, beyond], axis=1)
    for chunk in range(chunks):
        pair = []
        for core in range(2):
            start = (chunk * 2 + core) * width
            part = jnp.concatenate(
                [
                    jnp.dot(
                        pre, inputs[:, start : start + lanes], preferred_element_type=jnp.float32
                    ),
                    jnp.dot(
                        activation,
                        cotan[:, start : start + lanes],
                        preferred_element_type=jnp.float32,
                    ),
                ],
                axis=0,
            )
            pair.append(part.astype(jnp.bfloat16))

        @pl.when(core_ref[0] == 0)
        def _():
            mine_ref[chunk] = pair[0]
            other_ref[chunk] = pair[1]

        @pl.when(core_ref[0] == 1)
        def _():
            mine_ref[chunk] = pair[1]
            other_ref[chunk] = pair[0]


def shards(tokens, cotangent, gates, route_ids, w_gate, w_up, w_down):
    device_count = lax.axis_size("expert")
    replicas = lax.axis_size("dp")
    pieces = device_count // EXPERTS
    token_count, feature_count = tokens.shape
    hidden = w_gate.shape[0]
    chips = replicas // 2
    width = feature_count // replicas
    lanes = -(-width // 128) * 128
    vmem = pl.BlockSpec(memory_space=pltpu.VMEM)
    send, table = pl.pallas_call(
        select_kernel,
        out_shape=(
            jax.ShapeDtypeStruct((EXPERTS, pieces, CAP, 2 * feature_count), jnp.bfloat16),
            jax.ShapeDtypeStruct((EXPERTS * CAP, token_count), jnp.bfloat16),
        ),
        in_specs=[vmem] * 4,
        out_specs=(pl.BlockSpec(memory_space=pltpu.HBM), vmem),
        scratch_shapes=[
            pltpu.VMEM((EXPERTS, CAP, 2 * feature_count), jnp.bfloat16),
            pltpu.SemaphoreType.DMA((pieces,)),
        ],
        compiler_params=pltpu.CompilerParams(vmem_limit_bytes=16 * 2**20),
    )(route_ids.T, gates.T, tokens, cotangent)
    arrived = lax.all_to_all(
        send.reshape(device_count, CAP, 2 * feature_count),
        "expert",
        split_axis=0,
        concat_axis=0,
        tiled=True,
    )
    core = (lax.axis_index("dp") % 2).astype(jnp.int32).reshape(1)
    mine, other, pre = pl.pallas_call(
        functools.partial(grads_kernel, width),
        out_shape=(
            jax.ShapeDtypeStruct((chips, 3 * hidden, lanes), jnp.bfloat16),
            jax.ShapeDtypeStruct((chips, 3 * hidden, lanes), jnp.bfloat16),
            jax.ShapeDtypeStruct((2 * hidden, device_count * CAP), jnp.bfloat16),
        ),
        in_specs=[pl.BlockSpec(memory_space=pltpu.SMEM)] + [vmem] * 4,
        out_specs=(vmem, vmem, vmem),
        compiler_params=pltpu.CompilerParams(vmem_limit_bytes=40 * 2**20),
    )(core, arrived, w_gate, w_up, w_down)
    swap = [(i, i ^ 1) for i in range(replicas)]
    theirs = lax.ppermute(other, "dp", swap)
    chip_sum = (mine.astype(jnp.float32) + theirs.astype(jnp.float32)).astype(jnp.bfloat16)
    chip_sum, pre = lax.optimization_barrier((chip_sum, pre))
    same_core = [[2 * x + c for x in range(chips)] for c in range(2)]
    summed = lax.psum_scatter(
        chip_sum.reshape(chips * 3 * hidden, lanes),
        "dp",
        scatter_dimension=0,
        axis_index_groups=same_core,
        tiled=True,
    )
    down_first = (((0,), (0,)), ((), ()))
    partial = lax.dot_general(pre[:hidden], w_gate, down_first, preferred_element_type=jnp.float32)
    partial = partial + lax.dot_general(
        pre[hidden:], w_up, down_first, preferred_element_type=jnp.float32
    )
    piece_grad = partial.astype(jnp.bfloat16).reshape(device_count, CAP, feature_count)
    returned = lax.all_to_all(piece_grad, "expert", split_axis=0, concat_axis=0, tiled=True)
    returned_rows = returned.reshape(device_count * CAP, feature_count)
    pair_table = jnp.broadcast_to(
        table.reshape(EXPERTS, 1, CAP, token_count), (EXPERTS, pieces, CAP, token_count)
    ).reshape(device_count * CAP, token_count)
    grad_tokens = jnp.dot(pair_table.T, returned_rows, preferred_element_type=jnp.float32).astype(
        jnp.bfloat16
    )
    return (
        grad_tokens,
        summed[:hidden, :width],
        summed[hidden : 2 * hidden, :width],
        summed[2 * hidden :, :width],
    )


def solution(mesh):
    in_specs = (
        P(("expert", "dp"), None),
        P(("expert", "dp"), None),
        P(("expert", "dp"), None),
        P(("expert", "dp"), None),
        P("expert", None),
        P("expert", None),
        P("expert", None),
    )
    out_specs = (P(("expert", "dp"), None), P("expert", "dp"), P("expert", "dp"), P("expert", "dp"))
    return jax.shard_map(shards, mesh=mesh, in_specs=in_specs, out_specs=out_specs, check_vma=False)
```

```python
import functools

import jax
import jax.numpy as jnp
from jax import lax
from jax.experimental import pallas as pl
from jax.experimental.pallas import tpu as pltpu
from jax.sharding import PartitionSpec as P

EXPERTS = 4
CAP = 2


def select_kernel(
    ids_hbm, gates_hbm, tokens_hbm, cotan_hbm, send_ref, table_ref, ids_ref, gates_ref, tokens_ref,
    cotan_ref, rows_ref, in_sems, out_sems,
):
    slots, tokens = table_ref.shape
    loads = [
        pltpu.make_async_copy(source, target, in_sems.at[index])
        for index, (source, target) in enumerate(
            (
                (ids_hbm, ids_ref),
                (gates_hbm, gates_ref),
                (tokens_hbm, tokens_ref),
                (cotan_hbm, cotan_ref),
            )
        )
    ]
    for load in loads:
        load.start()
    slot = lax.broadcasted_iota(jnp.int32, (slots, tokens), 0)
    expert, place = slot // CAP, slot % CAP
    earlier = lax.broadcasted_iota(jnp.int32, (tokens, tokens), 0) < lax.broadcasted_iota(
        jnp.int32, (tokens, tokens), 1
    )
    earlier = jnp.where(earlier, 1.0, 0.0).astype(jnp.bfloat16)
    loads[0].wait()
    first = ids_ref[0:1, :] == expert
    second = ids_ref[1:2, :] == expert
    named = jnp.where(first | second, 1.0, 0.0)
    before = jnp.dot(named.astype(jnp.bfloat16), earlier, preferred_element_type=jnp.float32)
    table = jnp.where(before == place.astype(jnp.float32), named, 0.0)
    table_ref[...] = table.astype(jnp.bfloat16)
    loads[1].wait()
    gates = gates_ref[...].astype(jnp.float32)
    gated = table * jnp.where(first, gates[0:1, :], gates[1:2, :])
    stores = []
    for half, (weight, source_ref) in enumerate(((table, tokens_ref), (gated, cotan_ref))):
        loads[2 + half].wait()
        picked = jnp.dot(
            weight.astype(jnp.bfloat16), source_ref[...], preferred_element_type=jnp.float32
        )
        for e in range(EXPERTS):
            rows_ref[half, e] = picked[e * CAP : (e + 1) * CAP].astype(jnp.bfloat16)
        for piece in range(half, send_ref.shape[1], 2):
            store = pltpu.make_async_copy(
                rows_ref.at[half], send_ref.at[:, piece], out_sems.at[piece]
            )
            store.start()
            stores.append(store)
    for store in stores:
        store.wait()


def chunk_grads(width, lanes, core, pre, activation, inputs, cotan, out_ref):
    for chunk in range(out_ref.shape[0]):
        start = (chunk * 2 + core) * width
        part = jnp.concatenate(
            [
                jnp.dot(pre, inputs[:, start : start + lanes], preferred_element_type=jnp.float32),
                jnp.dot(
                    activation, cotan[:, start : start + lanes], preferred_element_type=jnp.float32
                ),
            ],
            axis=0,
        )
        out_ref[chunk] = part.astype(jnp.bfloat16)


def flatten(rows_ref, lanes):
    sources, cap, features = rows_ref.shape
    flat = rows_ref[...].reshape(sources * cap, features)
    beyond = jnp.zeros((sources * cap, lanes - features), jnp.bfloat16)
    return jnp.concatenate([flat, beyond], axis=1)


def project(weight_ref, rows):
    across = (((1,), (1,)), ((), ()))
    features = weight_ref.shape[1]
    return lax.dot_general(
        weight_ref[...], rows[:, :features], across, preferred_element_type=jnp.float32
    )


def first_kernel(
    odd_ref, rows_ref, gate_ref, up_hbm, down_hbm, flat_ref, up_ref, down_ref, forward_ref, back_ref,
    sems,
):
    load_up = pltpu.make_async_copy(up_hbm, up_ref, sems.at[0])
    load_down = pltpu.make_async_copy(down_hbm, down_ref, sems.at[1])
    load_up.start()
    load_down.start()
    flat_ref[...] = flatten(rows_ref, flat_ref.shape[1])

    @pl.when(odd_ref[0] == 0)
    def _():
        forward_ref[0] = project(gate_ref, flat_ref)

    load_up.wait()
    load_down.wait()

    @pl.when(odd_ref[0] == 0)
    def _():
        forward_ref[1] = project(up_ref, flat_ref)

    @pl.when(odd_ref[0] == 1)
    def _():
        back_ref[...] = project(down_ref, flat_ref)


def passes_kernel(
    width, core_ref, odd_ref, first_ref, low_ref, high_ref, gate_ref, up_ref, down_ref, done_forward_ref,
    done_back_ref, other_ref, pre_ref, act_ref, flat_ref, forward_ref, back_ref,
):
    lanes = other_ref.shape[2]
    half = flat_ref.shape[1] // 2
    odd = odd_ref[0]
    flat_ref[odd] = first_ref[...]
    flat_ref[1 - odd, :half] = flatten(low_ref, flat_ref.shape[2])
    flat_ref[1 - odd, half:] = flatten(high_ref, flat_ref.shape[2])

    @pl.when(odd == 0)
    def _():
        forward_ref[...] = done_forward_ref[...]
        back_ref[...] = project(down_ref, flat_ref.at[1])

    @pl.when(odd == 1)
    def _():
        forward_ref[0] = project(gate_ref, flat_ref.at[0])
        forward_ref[1] = project(up_ref, flat_ref.at[0])
        back_ref[...] = done_back_ref[...]

    gate_pre, up_pre, hidden = forward_ref[0], forward_ref[1], back_ref[...]
    sig = 1.0 / (1.0 + jnp.exp(-gate_pre))
    activation = (gate_pre * sig * up_pre).astype(jnp.bfloat16)
    grad_up = hidden * gate_pre * sig
    grad_gate = hidden * up_pre * sig * (1.0 + gate_pre * (1.0 - sig))
    pre = jnp.concatenate([grad_gate, grad_up], axis=0).astype(jnp.bfloat16)
    pre_ref[...] = pre
    act_ref[...] = activation
    for core in range(2):

        @pl.when(core_ref[0] == core)
        def _():
            chunk_grads(
                width, lanes, 1 - core, pre, activation, flat_ref[0], flat_ref[1], other_ref
            )


def own_kernel(width, core_ref, pre_ref, act_ref, flat_ref, mine_ref):
    lanes = mine_ref.shape[2]
    for core in range(2):

        @pl.when(core_ref[0] == core)
        def _():
            chunk_grads(
                width, lanes, core, pre_ref[...], act_ref[...], flat_ref[0], flat_ref[1], mine_ref
            )


def shards(tokens, cotangent, gates, route_ids, w_gate, w_up, w_down):
    device_count = lax.axis_size("expert")
    replicas = lax.axis_size("dp")
    pieces = device_count // EXPERTS
    token_count, feature_count = tokens.shape
    hidden = w_gate.shape[0]
    chips = replicas // 2
    width = feature_count // replicas
    lanes = -(-width // 128) * 128
    rows = device_count * CAP
    vmem = pl.BlockSpec(memory_space=pltpu.VMEM)
    smem = pl.BlockSpec(memory_space=pltpu.SMEM)
    hbm = pl.BlockSpec(memory_space=pltpu.HBM)
    in_hbm = functools.partial(pltpu.with_memory_space_constraint, memory_space=pltpu.HBM)
    send, table = pl.pallas_call(
        select_kernel,
        out_shape=(
            pltpu.HBM((EXPERTS, pieces, CAP, feature_count), jnp.bfloat16),
            jax.ShapeDtypeStruct((EXPERTS * CAP, token_count), jnp.bfloat16),
        ),
        in_specs=[hbm] * 4,
        out_specs=(hbm, vmem),
        scratch_shapes=[
            pltpu.VMEM((2, token_count), jnp.int32),
            pltpu.VMEM((2, token_count), jnp.bfloat16),
            pltpu.VMEM((token_count, feature_count), jnp.bfloat16),
            pltpu.VMEM((token_count, feature_count), jnp.bfloat16),
            pltpu.VMEM((2, EXPERTS, CAP, feature_count), jnp.bfloat16),
            pltpu.SemaphoreType.DMA((4,)),
            pltpu.SemaphoreType.DMA((pieces,)),
        ],
        compiler_params=pltpu.CompilerParams(vmem_limit_bytes=16 * 2**20),
    )(in_hbm(route_ids.T), in_hbm(gates.T), in_hbm(tokens), in_hbm(cotangent))
    arrived = lax.all_to_all(
        send.reshape(device_count, CAP, feature_count),
        "expert",
        split_axis=0,
        concat_axis=0,
        tiled=True,
    )
    ring = pieces // 2
    after = [(i, i // ring * ring + (i + 1) % ring) for i in range(device_count)]
    before = [(i, i // ring * ring + (i - 1) % ring) for i in range(device_count)]
    low = lax.ppermute(arrived[: device_count // 2], "expert", after)
    high = lax.ppermute(arrived[device_count // 2 :], "expert", before)
    odd = (lax.axis_index("expert") & 1).astype(jnp.int32).reshape(1)
    core = (lax.axis_index("dp") & 1).astype(jnp.int32).reshape(1)
    flat_lanes = feature_count + lanes // 2
    weight_shape = jax.ShapeDtypeStruct((hidden, feature_count), jnp.bfloat16)
    forward_shape = jax.ShapeDtypeStruct((2, hidden, rows), jnp.float32)
    back_shape = jax.ShapeDtypeStruct((hidden, rows), jnp.float32)
    first, up_here, down_here, forward, back = pl.pallas_call(
        first_kernel,
        out_shape=(
            jax.ShapeDtypeStruct((rows, flat_lanes), jnp.bfloat16),
            weight_shape,
            weight_shape,
            forward_shape,
            back_shape,
        ),
        in_specs=[smem, vmem, vmem, hbm, hbm],
        out_specs=(vmem,) * 5,
        scratch_shapes=[pltpu.SemaphoreType.DMA((2,))],
        compiler_params=pltpu.CompilerParams(vmem_limit_bytes=32 * 2**20),
        cost_estimate=pl.CostEstimate(
            flops=4 * hidden * rows * feature_count, bytes_accessed=8 * 2**20, transcendentals=0
        ),
    )(odd, arrived, w_gate, in_hbm(w_up), in_hbm(w_down))
    grads_shape = jax.ShapeDtypeStruct((chips, 3 * hidden, lanes), jnp.bfloat16)
    other, pre, activation, flat = pl.pallas_call(
        functools.partial(passes_kernel, width),
        out_shape=(
            grads_shape,
            jax.ShapeDtypeStruct((2 * hidden, rows), jnp.bfloat16),
            jax.ShapeDtypeStruct((hidden, rows), jnp.bfloat16),
            jax.ShapeDtypeStruct((2, rows, flat_lanes), jnp.bfloat16),
        ),
        in_specs=[smem, smem] + [vmem] * 8,
        out_specs=(vmem,) * 4,
        scratch_shapes=[
            pltpu.VMEM((2, hidden, rows), jnp.float32),
            pltpu.VMEM((hidden, rows), jnp.float32),
        ],
        compiler_params=pltpu.CompilerParams(vmem_limit_bytes=32 * 2**20),
    )(core, odd, first, low, high, w_gate, up_here, down_here, forward, back)
    swap = [(i, i ^ 1) for i in range(replicas)]
    theirs = lax.ppermute(other, "dp", swap)
    mine = pl.pallas_call(
        functools.partial(own_kernel, width),
        out_shape=grads_shape,
        in_specs=[smem] + [vmem] * 3,
        out_specs=vmem,
        compiler_params=pltpu.CompilerParams(vmem_limit_bytes=32 * 2**20),
        cost_estimate=pl.CostEstimate(
            flops=6 * hidden * rows * feature_count, bytes_accessed=4 * 2**20, transcendentals=0
        ),
    )(core, pre, activation, flat)
    chip_sum = (mine.astype(jnp.float32) + theirs.astype(jnp.float32)).astype(jnp.bfloat16)
    chip_sum, pre = lax.optimization_barrier((chip_sum, pre))
    same_core = [[2 * x + c for x in range(chips)] for c in range(2)]
    summed = lax.psum_scatter(
        chip_sum.reshape(chips * 3 * hidden, lanes),
        "dp",
        scatter_dimension=0,
        axis_index_groups=same_core,
        tiled=True,
    )
    down_first = (((0,), (0,)), ((), ()))
    partial = lax.dot_general(pre[:hidden], w_gate, down_first, preferred_element_type=jnp.float32)
    partial = partial + lax.dot_general(
        pre[hidden:], w_up, down_first, preferred_element_type=jnp.float32
    )
    piece_grad = partial.astype(jnp.bfloat16).reshape(device_count, CAP, feature_count)
    returned = lax.all_to_all(piece_grad, "expert", split_axis=0, concat_axis=0, tiled=True)
    returned_rows = returned.reshape(device_count * CAP, feature_count)
    pair_table = jnp.broadcast_to(
        table.reshape(EXPERTS, 1, CAP, token_count), (EXPERTS, pieces, CAP, token_count)
    ).reshape(device_count * CAP, token_count)
    grad_tokens = jnp.dot(pair_table.T, returned_rows, preferred_element_type=jnp.float32).astype(
        jnp.bfloat16
    )
    return (
        grad_tokens,
        summed[:hidden, :width],
        summed[hidden : 2 * hidden, :width],
        summed[2 * hidden :, :width],
    )


def solution(mesh):
    in_specs = (
        P(("expert", "dp"), None),
        P(("expert", "dp"), None),
        P(("expert", "dp"), None),
        P(("expert", "dp"), None),
        P("expert", None),
        P("expert", None),
        P("expert", None),
    )
    out_specs = (P(("expert", "dp"), None), P("expert", "dp"), P("expert", "dp"), P("expert", "dp"))
    return jax.shard_map(shards, mesh=mesh, in_specs=in_specs, out_specs=out_specs, check_vma=False)
```

```python
import functools

import jax
import jax.numpy as jnp
from jax import lax
from jax.experimental import pallas as pl
from jax.experimental.pallas import tpu as pltpu
from jax.sharding import PartitionSpec as P

EXPERTS = 4
CAP = 2


def select_kernel(
    ids_hbm, gates_hbm, tokens_hbm, cotan_hbm, send_ref, table_ref, ids_ref, gates_ref, tokens_ref,
    cotan_ref, rows_ref, in_sems, out_sems,
):
    slots, tokens = EXPERTS * CAP, table_ref.shape[1]
    loads = [
        pltpu.make_async_copy(source, target, in_sems.at[index])
        for index, (source, target) in enumerate(
            (
                (ids_hbm, ids_ref),
                (gates_hbm, gates_ref),
                (tokens_hbm, tokens_ref),
                (cotan_hbm, cotan_ref),
            )
        )
    ]
    for load in loads:
        load.start()
    slot = lax.broadcasted_iota(jnp.int32, (slots, tokens), 0)
    expert, place = slot // CAP, slot % CAP
    earlier = lax.broadcasted_iota(jnp.int32, (tokens, tokens), 0) < lax.broadcasted_iota(
        jnp.int32, (tokens, tokens), 1
    )
    earlier = jnp.where(earlier, 1.0, 0.0).astype(jnp.bfloat16)
    loads[0].wait()
    first = ids_ref[0:1, :] == expert
    second = ids_ref[1:2, :] == expert
    named = jnp.where(first | second, 1.0, 0.0)
    before = jnp.dot(named.astype(jnp.bfloat16), earlier, preferred_element_type=jnp.float32)
    table = jnp.where(before == place.astype(jnp.float32), named, 0.0)
    sub = lax.broadcasted_iota(jnp.int32, table_ref.shape, 0)
    per_expert = table_ref.shape[0] // EXPERTS
    repeated = jnp.zeros(table_ref.shape, jnp.float32)
    for e in range(EXPERTS):
        for p in range(CAP):
            here = (sub // per_expert == e) & (sub % CAP == p)
            repeated = jnp.where(here, table[e * CAP + p : e * CAP + p + 1, :], repeated)
    table_ref[...] = repeated.astype(jnp.bfloat16)
    loads[1].wait()
    gates = gates_ref[...].astype(jnp.float32)
    gated = table * jnp.where(first, gates[0:1, :], gates[1:2, :])
    stores = []
    for half, (weight, source_ref) in enumerate(((table, tokens_ref), (gated, cotan_ref))):
        loads[2 + half].wait()
        picked = jnp.dot(
            weight.astype(jnp.bfloat16), source_ref[...], preferred_element_type=jnp.float32
        )
        for e in range(EXPERTS):
            rows_ref[half, e] = picked[e * CAP : (e + 1) * CAP].astype(jnp.bfloat16)
        for piece in range(half, send_ref.shape[1], 2):
            store = pltpu.make_async_copy(
                rows_ref.at[half], send_ref.at[:, piece], out_sems.at[piece]
            )
            store.start()
            stores.append(store)
    for store in stores:
        store.wait()


def chunk_grads(width, core, pre, activation, inputs, cotan, out_ref):
    chunks, _, lanes = out_ref.shape
    for chunk in range(chunks):
        start = (chunk * 2 + core) * width
        part = jnp.concatenate(
            [
                jnp.dot(pre, inputs[:, start : start + lanes], preferred_element_type=jnp.float32),
                jnp.dot(
                    activation, cotan[:, start : start + lanes], preferred_element_type=jnp.float32
                ),
            ],
            axis=0,
        )
        out_ref[chunk] = part.astype(jnp.bfloat16)


def halve_kernel(rows_ref, low_ref, high_ref):
    half = low_ref.shape[0]
    low_ref[...] = rows_ref[:half]
    high_ref[...] = rows_ref[half:]


def flatten(rows_ref, lanes):
    sources, cap, features = rows_ref.shape
    flat = rows_ref[...].reshape(sources * cap, features)
    beyond = jnp.zeros((sources * cap, lanes - features), jnp.bfloat16)
    return jnp.concatenate([flat, beyond], axis=1)


def project(weight_ref, rows):
    across = (((1,), (1,)), ((), ()))
    features = weight_ref.shape[1]
    return lax.dot_general(
        weight_ref[...], rows[:, :features], across, preferred_element_type=jnp.float32
    )


def first_kernel(
    piece_at_ref, rows_ref, gate_ref, up_hbm, down_hbm, flat_ref, up_ref, down_ref, forward_ref, back_ref,
    sems,
):
    load_up = pltpu.make_async_copy(up_hbm, up_ref, sems.at[0])
    load_down = pltpu.make_async_copy(down_hbm, down_ref, sems.at[1])
    load_up.start()
    load_down.start()
    flat_ref[...] = flatten(rows_ref, flat_ref.shape[1])

    @pl.when(piece_at_ref[0] & 1 == 0)
    def _():
        forward_ref[0] = project(gate_ref, flat_ref)

    load_up.wait()
    load_down.wait()

    @pl.when(piece_at_ref[0] & 1 == 0)
    def _():
        forward_ref[1] = project(up_ref, flat_ref)

    @pl.when(piece_at_ref[0] & 1 == 1)
    def _():
        back_ref[...] = project(down_ref, flat_ref)


def passes_kernel(
    width, replica_ref, piece_at_ref, first_ref, low_ref, high_ref, gate_ref, up_ref, down_ref, done_forward_ref,
    done_back_ref, other_ref, pre_ref, act_ref, flat_ref, forward_ref, back_ref,
):
    half = flat_ref.shape[1] // 2
    odd = piece_at_ref[0] & 1
    flat_ref[odd] = first_ref[...]
    flat_ref[1 - odd, :half] = flatten(low_ref, flat_ref.shape[2])
    flat_ref[1 - odd, half:] = flatten(high_ref, flat_ref.shape[2])

    @pl.when(odd == 0)
    def _():
        forward_ref[...] = done_forward_ref[...]
        back_ref[...] = project(down_ref, flat_ref.at[1])

    @pl.when(odd == 1)
    def _():
        forward_ref[0] = project(gate_ref, flat_ref.at[0])
        forward_ref[1] = project(up_ref, flat_ref.at[0])
        back_ref[...] = done_back_ref[...]

    gate_pre, up_pre, hidden = forward_ref[0], forward_ref[1], back_ref[...]
    sig = 1.0 / (1.0 + jnp.exp(-gate_pre))
    activation = (gate_pre * sig * up_pre).astype(jnp.bfloat16)
    grad_up = hidden * gate_pre * sig
    grad_gate = hidden * up_pre * sig * (1.0 + gate_pre * (1.0 - sig))
    pre = jnp.concatenate([grad_gate, grad_up], axis=0).astype(jnp.bfloat16)
    pre_ref[...] = pre
    act_ref[...] = activation
    for core in range(2):

        @pl.when(replica_ref[0] & 1 == core)
        def _():
            chunk_grads(width, 1 - core, pre, activation, flat_ref[0], flat_ref[1], other_ref)


def own_kernel(width, replica_ref, pre_ref, act_ref, flat_ref, mine_ref):
    for core in range(2):

        @pl.when(replica_ref[0] & 1 == core)
        def _():
            chunk_grads(width, core, pre_ref[...], act_ref[...], flat_ref[0], flat_ref[1], mine_ref)


def piece_kernel(pre_ref, gate_ref, up_ref, piece_hbm, piece_ref, sem):
    hidden = gate_ref.shape[0]
    pre = pre_ref[...].astype(jnp.float32)
    down = (((0,), (0,)), ((), ()))
    piece = lax.dot_general(
        pre[:hidden].astype(jnp.bfloat16), gate_ref[...], down, preferred_element_type=jnp.float32
    ) + lax.dot_general(
        pre[hidden:].astype(jnp.bfloat16), up_ref[...], down, preferred_element_type=jnp.float32
    )
    piece_ref[...] = piece.astype(jnp.bfloat16).reshape(piece_ref.shape)
    store = pltpu.make_async_copy(piece_ref, piece_hbm, sem)
    store.start()
    store.wait()


def combine_kernel(table_ref, rows_ref, tokens_ref):
    flat = rows_ref[...].reshape(table_ref.shape[0], tokens_ref.shape[1])
    total = lax.dot_general(
        table_ref[...], flat, (((0,), (0,)), ((), ())), preferred_element_type=jnp.float32
    )
    tokens_ref[...] = total.astype(jnp.bfloat16)


def added(first, second):
    return (first.astype(jnp.float32) + second.astype(jnp.float32)).astype(jnp.bfloat16)


def chip_kernel(replica_ref, mine_ref, theirs_ref, *out_refs):
    chips = len(out_refs)
    for distance, out_ref in enumerate(out_refs):
        chunk = ((replica_ref[0] >> 1) + distance) & (chips - 1)
        out_ref[...] = added(mine_ref[chunk], theirs_ref[chunk])


def add_kernel(got_ref, own_ref, sum_ref):
    sum_ref[...] = added(got_ref[...], own_ref[...])


def total_kernel(up_ring_ref, down_ring_ref, own_ref, gate_ref, up_ref, down_ref):
    hidden, width = gate_ref.shape
    total = up_ring_ref[...].astype(jnp.float32) + down_ring_ref[...].astype(jnp.float32)
    total = total + own_ref[...].astype(jnp.float32)
    for index, out_ref in enumerate((gate_ref, up_ref, down_ref)):
        rows = total[index * hidden : (index + 1) * hidden]
        out_ref[...] = rows[:, :width].astype(jnp.bfloat16)


def shards(tokens, cotangent, gates, route_ids, w_gate, w_up, w_down):
    device_count = lax.axis_size("expert")
    replicas = lax.axis_size("dp")
    pieces = device_count // EXPERTS
    token_count, feature_count = tokens.shape
    hidden = w_gate.shape[0]
    chips = replicas // 2
    width = feature_count // replicas
    lanes = -(-width // 128) * 128
    rows = device_count * CAP
    vmem = pl.BlockSpec(memory_space=pltpu.VMEM)
    smem = pl.BlockSpec(memory_space=pltpu.SMEM)
    hbm = pl.BlockSpec(memory_space=pltpu.HBM)
    in_hbm = functools.partial(pltpu.with_memory_space_constraint, memory_space=pltpu.HBM)
    send, table = pl.pallas_call(
        select_kernel,
        out_shape=(
            pltpu.HBM((EXPERTS, pieces, CAP, feature_count), jnp.bfloat16),
            jax.ShapeDtypeStruct((rows, token_count), jnp.bfloat16),
        ),
        in_specs=[hbm] * 4,
        out_specs=(hbm, vmem),
        scratch_shapes=[
            pltpu.VMEM((2, token_count), jnp.int32),
            pltpu.VMEM((2, token_count), jnp.bfloat16),
            pltpu.VMEM((token_count, feature_count), jnp.bfloat16),
            pltpu.VMEM((token_count, feature_count), jnp.bfloat16),
            pltpu.VMEM((2, EXPERTS, CAP, feature_count), jnp.bfloat16),
            pltpu.SemaphoreType.DMA((4,)),
            pltpu.SemaphoreType.DMA((pieces,)),
        ],
        compiler_params=pltpu.CompilerParams(vmem_limit_bytes=16 * 2**20),
    )(in_hbm(route_ids.T), in_hbm(gates.T), in_hbm(tokens), in_hbm(cotangent))
    arrived = lax.all_to_all(
        send.reshape(device_count, CAP, feature_count),
        "expert",
        split_axis=0,
        concat_axis=0,
        tiled=True,
    )
    ring = pieces // 2
    after = [(i, i // ring * ring + (i + 1) % ring) for i in range(device_count)]
    before = [(i, i // ring * ring + (i - 1) % ring) for i in range(device_count)]
    half_shape = jax.ShapeDtypeStruct((device_count // 2, CAP, feature_count), jnp.bfloat16)
    low, high = pl.pallas_call(
        halve_kernel,
        out_shape=(half_shape, half_shape),
        in_specs=[vmem],
        out_specs=(vmem, vmem),
        compiler_params=pltpu.CompilerParams(vmem_limit_bytes=12 * 2**20),
    )(arrived)
    low = lax.ppermute(low, "expert", after)
    high = lax.ppermute(high, "expert", before)
    piece_at = lax.axis_index("expert").astype(jnp.int32).reshape(1)
    replica = lax.axis_index("dp").astype(jnp.int32).reshape(1)
    flat_lanes = feature_count + lanes // 2
    weight_shape = jax.ShapeDtypeStruct((hidden, feature_count), jnp.bfloat16)
    forward_shape = jax.ShapeDtypeStruct((2, hidden, rows), jnp.float32)
    back_shape = jax.ShapeDtypeStruct((hidden, rows), jnp.float32)
    first, up_here, down_here, forward, back = pl.pallas_call(
        first_kernel,
        out_shape=(
            jax.ShapeDtypeStruct((rows, flat_lanes), jnp.bfloat16),
            weight_shape,
            weight_shape,
            forward_shape,
            back_shape,
        ),
        in_specs=[smem, vmem, vmem, hbm, hbm],
        out_specs=(vmem,) * 5,
        scratch_shapes=[pltpu.SemaphoreType.DMA((2,))],
        compiler_params=pltpu.CompilerParams(vmem_limit_bytes=12 * 2**20),
        cost_estimate=pl.CostEstimate(
            flops=4 * hidden * rows * feature_count, bytes_accessed=8 * 2**20, transcendentals=0
        ),
    )(piece_at, arrived, w_gate, in_hbm(w_up), in_hbm(w_down))
    grads_shape = jax.ShapeDtypeStruct((chips, 3 * hidden, lanes), jnp.bfloat16)
    other, pre, activation, flat = pl.pallas_call(
        functools.partial(passes_kernel, width),
        out_shape=(
            grads_shape,
            jax.ShapeDtypeStruct((2 * hidden, rows), jnp.bfloat16),
            jax.ShapeDtypeStruct((hidden, rows), jnp.bfloat16),
            jax.ShapeDtypeStruct((2, rows, flat_lanes), jnp.bfloat16),
        ),
        in_specs=[smem, smem] + [vmem] * 8,
        out_specs=(vmem,) * 4,
        scratch_shapes=[
            pltpu.VMEM((2, hidden, rows), jnp.float32),
            pltpu.VMEM((hidden, rows), jnp.float32),
        ],
        compiler_params=pltpu.CompilerParams(vmem_limit_bytes=12 * 2**20),
    )(replica, piece_at, first, low, high, w_gate, up_here, down_here, forward, back)
    swap = [(i, i ^ 1) for i in range(replicas)]
    theirs = lax.ppermute(other, "dp", swap)
    mine = pl.pallas_call(
        functools.partial(own_kernel, width),
        out_shape=grads_shape,
        in_specs=[smem] + [vmem] * 3,
        out_specs=vmem,
        compiler_params=pltpu.CompilerParams(vmem_limit_bytes=12 * 2**20),
        cost_estimate=pl.CostEstimate(
            flops=6 * hidden * rows * feature_count, bytes_accessed=4 * 2**20, transcendentals=0
        ),
    )(replica, pre, activation, flat)
    chunk_shape = jax.ShapeDtypeStruct((3 * hidden, lanes), jnp.bfloat16)
    small = pltpu.CompilerParams(vmem_limit_bytes=12 * 2**20)
    chunks = pl.pallas_call(
        chip_kernel,
        out_shape=(chunk_shape,) * chips,
        in_specs=[smem, vmem, vmem],
        out_specs=(vmem,) * chips,
        compiler_params=small,
    )(replica, mine, theirs)
    add = pl.pallas_call(
        add_kernel,
        out_shape=chunk_shape,
        in_specs=[vmem, vmem],
        out_specs=vmem,
        compiler_params=small,
    )
    far = chips // 2
    chunks = list(chunks)
    chunks[far], pre = lax.optimization_barrier((chunks[far], pre))
    piece_grad = pl.pallas_call(
        piece_kernel,
        out_shape=pltpu.HBM((device_count, CAP, feature_count), jnp.bfloat16),
        in_specs=[vmem] * 3,
        out_specs=hbm,
        scratch_shapes=[
            pltpu.VMEM((device_count, CAP, feature_count), jnp.bfloat16),
            pltpu.SemaphoreType.DMA(()),
        ],
        compiler_params=pltpu.CompilerParams(vmem_limit_bytes=12 * 2**20),
        cost_estimate=pl.CostEstimate(
            flops=4 * hidden * rows * feature_count, bytes_accessed=4 * 2**20, transcendentals=0
        ),
    )(pre, w_gate, up_here)
    ahead = [(i, (i + 2) % replicas) for i in range(replicas)]
    back = [(i, (i - 2) % replicas) for i in range(replicas)]
    rising = lax.ppermute(chunks[far], "dp", ahead)
    falling = lax.ppermute(chunks[chips - far + 1], "dp", back)
    for distance in range(far - 1, 0, -1):
        rising = lax.ppermute(add(rising, chunks[distance]), "dp", ahead)
        if distance > 1:
            falling = lax.ppermute(add(falling, chunks[chips - distance + 1]), "dp", back)
    returned = lax.all_to_all(piece_grad, "expert", split_axis=0, concat_axis=0, tiled=True)
    grad_tokens = pl.pallas_call(
        combine_kernel,
        out_shape=jax.ShapeDtypeStruct((token_count, feature_count), jnp.bfloat16),
        in_specs=[vmem, vmem],
        out_specs=vmem,
        compiler_params=small,
        cost_estimate=pl.CostEstimate(
            flops=2 * rows * token_count * feature_count,
            bytes_accessed=2 * 2**20,
            transcendentals=0,
        ),
    )(table, returned)
    rising, grad_tokens = lax.optimization_barrier((rising, grad_tokens))
    owned = jax.ShapeDtypeStruct((hidden, width), jnp.bfloat16)
    grads = pl.pallas_call(
        total_kernel,
        out_shape=(owned,) * 3,
        in_specs=[vmem] * 3,
        out_specs=(vmem,) * 3,
        compiler_params=small,
    )(rising, falling, chunks[0])
    return (grad_tokens, *grads)


def solution(mesh):
    in_specs = (
        P(("expert", "dp"), None),
        P(("expert", "dp"), None),
        P(("expert", "dp"), None),
        P(("expert", "dp"), None),
        P("expert", None),
        P("expert", None),
        P("expert", None),
    )
    out_specs = (P(("expert", "dp"), None), P("expert", "dp"), P("expert", "dp"), P("expert", "dp"))
    return jax.shard_map(shards, mesh=mesh, in_specs=in_specs, out_specs=out_specs, check_vma=False)
```

```python
import functools

import jax
import jax.numpy as jnp
from jax import lax
from jax.experimental import pallas as pl
from jax.experimental.pallas import tpu as pltpu
from jax.sharding import PartitionSpec as P

EXPERTS = 4
CAP = 2


def select_kernel(
    ids_hbm, gates_hbm, tokens_hbm, cotan_hbm, send_ref, table_ref, ids_ref, gates_ref, tokens_ref,
    cotan_ref, rows_ref, in_sems, out_sems,
):
    slots, tokens = EXPERTS * CAP, table_ref.shape[1]
    loads = [
        pltpu.make_async_copy(source, target, in_sems.at[index])
        for index, (source, target) in enumerate(
            (
                (ids_hbm, ids_ref),
                (gates_hbm, gates_ref),
                (tokens_hbm, tokens_ref),
                (cotan_hbm, cotan_ref),
            )
        )
    ]
    for load in loads:
        load.start()
    slot = lax.broadcasted_iota(jnp.int32, (slots, tokens), 0)
    expert, place = slot // CAP, slot % CAP
    earlier = lax.broadcasted_iota(jnp.int32, (tokens, tokens), 0) < lax.broadcasted_iota(
        jnp.int32, (tokens, tokens), 1
    )
    earlier = jnp.where(earlier, 1.0, 0.0).astype(jnp.bfloat16)
    loads[0].wait()
    first = ids_ref[0:1, :] == expert
    second = ids_ref[1:2, :] == expert
    named = jnp.where(first | second, 1.0, 0.0)
    before = jnp.dot(named.astype(jnp.bfloat16), earlier, preferred_element_type=jnp.float32)
    table = jnp.where(before == place.astype(jnp.float32), named, 0.0)
    sub = lax.broadcasted_iota(jnp.int32, table_ref.shape, 0)
    per_expert = table_ref.shape[0] // EXPERTS
    repeated = jnp.zeros(table_ref.shape, jnp.float32)
    for e in range(EXPERTS):
        for p in range(CAP):
            here = (sub // per_expert == e) & (sub % CAP == p)
            repeated = jnp.where(here, table[e * CAP + p : e * CAP + p + 1, :], repeated)
    table_ref[...] = repeated.astype(jnp.bfloat16)
    loads[1].wait()
    gates = gates_ref[...].astype(jnp.float32)
    gated = table * jnp.where(first, gates[0:1, :], gates[1:2, :])
    stores = []
    for half, (weight, source_ref) in enumerate(((table, tokens_ref), (gated, cotan_ref))):
        loads[2 + half].wait()
        picked = jnp.dot(
            weight.astype(jnp.bfloat16), source_ref[...], preferred_element_type=jnp.float32
        )
        for e in range(EXPERTS):
            rows_ref[half, e] = picked[e * CAP : (e + 1) * CAP].astype(jnp.bfloat16)
        for piece in range(half, send_ref.shape[1], 2):
            store = pltpu.make_async_copy(
                rows_ref.at[half], send_ref.at[:, piece], out_sems.at[piece]
            )
            store.start()
            stores.append(store)
    for store in stores:
        store.wait()


def chunk_grads(width, core, pre, activation, inputs, cotan, out_ref):
    chunks, _, lanes = out_ref.shape
    for chunk in range(chunks):
        start = (chunk * 2 + core) * width
        part = jnp.concatenate(
            [
                jnp.dot(pre, inputs[:, start : start + lanes], preferred_element_type=jnp.float32),
                jnp.dot(
                    activation, cotan[:, start : start + lanes], preferred_element_type=jnp.float32
                ),
            ],
            axis=0,
        )
        out_ref[chunk] = part.astype(jnp.bfloat16)


def part_kernel(start, rows_ref, part_ref):
    part_ref[...] = rows_ref[start : start + part_ref.shape[0]]


def flatten(rows_ref, lanes):
    sources, cap, features = rows_ref.shape
    flat = rows_ref[...].reshape(sources * cap, features)
    beyond = jnp.zeros((sources * cap, lanes - features), jnp.bfloat16)
    return jnp.concatenate([flat, beyond], axis=1)


def project(weight_ref, rows):
    across = (((1,), (1,)), ((), ()))
    features = weight_ref.shape[1]
    return lax.dot_general(
        weight_ref[...], rows[:, :features], across, preferred_element_type=jnp.float32
    )


def first_kernel(
    piece_at_ref, rows_ref, gate_ref, up_hbm, down_hbm, flat_ref, up_ref, down_ref, forward_ref, back_ref,
    sems,
):
    load_up = pltpu.make_async_copy(up_hbm, up_ref, sems.at[0])
    load_down = pltpu.make_async_copy(down_hbm, down_ref, sems.at[1])
    load_up.start()
    load_down.start()
    flat_ref[...] = flatten(rows_ref, flat_ref.shape[1])

    @pl.when(piece_at_ref[0] & 1 == 0)
    def _():
        forward_ref[0] = project(gate_ref, flat_ref)

    load_up.wait()
    load_down.wait()

    @pl.when(piece_at_ref[0] & 1 == 0)
    def _():
        forward_ref[1] = project(up_ref, flat_ref)

    @pl.when(piece_at_ref[0] & 1 == 1)
    def _():
        back_ref[...] = project(down_ref, flat_ref)


def passes_kernel(
    width, replica_ref, piece_at_ref, first_ref, low_ref, high_ref, gate_ref, up_ref, down_ref, done_forward_ref,
    done_back_ref, other_ref, pre_ref, act_ref, flat_ref, forward_ref, back_ref,
):
    half = CAP * low_ref.shape[0]
    odd = piece_at_ref[0] & 1
    flat_ref[odd] = first_ref[...]
    flat_ref[1 - odd, :half] = flatten(low_ref, flat_ref.shape[2])
    flat_ref[1 - odd, half:] = flatten(high_ref, flat_ref.shape[2])

    @pl.when(odd == 0)
    def _():
        forward_ref[...] = done_forward_ref[...]
        back_ref[...] = project(down_ref, flat_ref.at[1])

    @pl.when(odd == 1)
    def _():
        forward_ref[0] = project(gate_ref, flat_ref.at[0])
        forward_ref[1] = project(up_ref, flat_ref.at[0])
        back_ref[...] = done_back_ref[...]

    gate_pre, up_pre, hidden = forward_ref[0], forward_ref[1], back_ref[...]
    sig = 1.0 / (1.0 + jnp.exp(-gate_pre))
    activation = (gate_pre * sig * up_pre).astype(jnp.bfloat16)
    grad_up = hidden * gate_pre * sig
    grad_gate = hidden * up_pre * sig * (1.0 + gate_pre * (1.0 - sig))
    pre = jnp.concatenate([grad_gate, grad_up], axis=0).astype(jnp.bfloat16)
    pre_ref[...] = pre
    act_ref[...] = activation
    for core in range(2):

        @pl.when(replica_ref[0] & 1 == core)
        def _():
            chunk_grads(width, 1 - core, pre, activation, flat_ref[0], flat_ref[1], other_ref)


def own_kernel(width, replica_ref, pre_ref, act_ref, flat_ref, mine_ref):
    for core in range(2):

        @pl.when(replica_ref[0] & 1 == core)
        def _():
            chunk_grads(width, core, pre_ref[...], act_ref[...], flat_ref[0], flat_ref[1], mine_ref)


def piece_kernel(pre_ref, gate_ref, up_ref, piece_hbm, piece_ref, sem):
    hidden = gate_ref.shape[0]
    pre = pre_ref[...].astype(jnp.float32)
    down = (((0,), (0,)), ((), ()))
    piece = lax.dot_general(
        pre[:hidden].astype(jnp.bfloat16), gate_ref[...], down, preferred_element_type=jnp.float32
    ) + lax.dot_general(
        pre[hidden:].astype(jnp.bfloat16), up_ref[...], down, preferred_element_type=jnp.float32
    )
    piece_ref[...] = piece.astype(jnp.bfloat16).reshape(piece_ref.shape)
    store = pltpu.make_async_copy(piece_ref, piece_hbm, sem)
    store.start()
    store.wait()


def combine_kernel(table_ref, rows_ref, tokens_ref):
    flat = rows_ref[...].reshape(table_ref.shape[0], tokens_ref.shape[1])
    total = lax.dot_general(
        table_ref[...], flat, (((0,), (0,)), ((), ())), preferred_element_type=jnp.float32
    )
    tokens_ref[...] = total.astype(jnp.bfloat16)


def added(first, second):
    return (first.astype(jnp.float32) + second.astype(jnp.float32)).astype(jnp.bfloat16)


def chip_kernel(replica_ref, mine_ref, theirs_ref, *out_refs):
    chips = len(out_refs)
    for distance, out_ref in enumerate(out_refs):
        chunk = ((replica_ref[0] >> 1) + distance) & (chips - 1)
        out_ref[...] = added(mine_ref[chunk], theirs_ref[chunk])


def add_kernel(got_ref, own_ref, sum_ref):
    sum_ref[...] = added(got_ref[...], own_ref[...])


def total_kernel(up_ring_ref, down_ring_ref, own_ref, gate_ref, up_ref, down_ref):
    hidden, width = gate_ref.shape
    total = up_ring_ref[...].astype(jnp.float32) + down_ring_ref[...].astype(jnp.float32)
    total = total + own_ref[...].astype(jnp.float32)
    for index, out_ref in enumerate((gate_ref, up_ref, down_ref)):
        rows = total[index * hidden : (index + 1) * hidden]
        out_ref[...] = rows[:, :width].astype(jnp.bfloat16)


def shards(tokens, cotangent, gates, route_ids, w_gate, w_up, w_down):
    device_count = lax.axis_size("expert")
    replicas = lax.axis_size("dp")
    pieces = device_count // EXPERTS
    token_count, feature_count = tokens.shape
    hidden = w_gate.shape[0]
    chips = replicas // 2
    width = feature_count // replicas
    lanes = -(-width // 128) * 128
    rows = device_count * CAP
    vmem = pl.BlockSpec(memory_space=pltpu.VMEM)
    smem = pl.BlockSpec(memory_space=pltpu.SMEM)
    hbm = pl.BlockSpec(memory_space=pltpu.HBM)
    in_hbm = functools.partial(pltpu.with_memory_space_constraint, memory_space=pltpu.HBM)
    send, table = pl.pallas_call(
        select_kernel,
        out_shape=(
            pltpu.HBM((EXPERTS, pieces, CAP, feature_count), jnp.bfloat16),
            jax.ShapeDtypeStruct((rows, token_count), jnp.bfloat16),
        ),
        in_specs=[hbm] * 4,
        out_specs=(hbm, vmem),
        scratch_shapes=[
            pltpu.VMEM((2, token_count), jnp.int32),
            pltpu.VMEM((2, token_count), jnp.bfloat16),
            pltpu.VMEM((token_count, feature_count), jnp.bfloat16),
            pltpu.VMEM((token_count, feature_count), jnp.bfloat16),
            pltpu.VMEM((2, EXPERTS, CAP, feature_count), jnp.bfloat16),
            pltpu.SemaphoreType.DMA((4,)),
            pltpu.SemaphoreType.DMA((pieces,)),
        ],
        compiler_params=pltpu.CompilerParams(vmem_limit_bytes=16 * 2**20),
    )(in_hbm(route_ids.T), in_hbm(gates.T), in_hbm(tokens), in_hbm(cotangent))
    arrived = lax.all_to_all(
        send.reshape(device_count, CAP, feature_count),
        "expert",
        split_axis=0,
        concat_axis=0,
        tiled=True,
    )
    ring = pieces // 2
    after = [(i, i // ring * ring + (i + 1) % ring) for i in range(device_count)]
    before = [(i, i // ring * ring + (i - 1) % ring) for i in range(device_count)]
    split = device_count * 5 // 8

    def part(start, size):
        return pl.pallas_call(
            functools.partial(part_kernel, start),
            out_shape=jax.ShapeDtypeStruct((size, CAP, feature_count), jnp.bfloat16),
            in_specs=[vmem],
            out_specs=vmem,
            compiler_params=pltpu.CompilerParams(vmem_limit_bytes=12 * 2**20),
        )(arrived)

    low, high = part(0, split), part(split, device_count - split)
    low = lax.ppermute(low, "expert", after)
    high = lax.ppermute(high, "expert", before)
    piece_at = lax.axis_index("expert").astype(jnp.int32).reshape(1)
    replica = lax.axis_index("dp").astype(jnp.int32).reshape(1)
    flat_lanes = feature_count + lanes // 2
    weight_shape = jax.ShapeDtypeStruct((hidden, feature_count), jnp.bfloat16)
    forward_shape = jax.ShapeDtypeStruct((2, hidden, rows), jnp.float32)
    back_shape = jax.ShapeDtypeStruct((hidden, rows), jnp.float32)
    first, up_here, down_here, forward, back = pl.pallas_call(
        first_kernel,
        out_shape=(
            jax.ShapeDtypeStruct((rows, flat_lanes), jnp.bfloat16),
            weight_shape,
            weight_shape,
            forward_shape,
            back_shape,
        ),
        in_specs=[smem, vmem, vmem, hbm, hbm],
        out_specs=(vmem,) * 5,
        scratch_shapes=[pltpu.SemaphoreType.DMA((2,))],
        compiler_params=pltpu.CompilerParams(vmem_limit_bytes=12 * 2**20),
        cost_estimate=pl.CostEstimate(
            flops=4 * hidden * rows * feature_count, bytes_accessed=8 * 2**20, transcendentals=0
        ),
    )(piece_at, arrived, w_gate, in_hbm(w_up), in_hbm(w_down))
    grads_shape = jax.ShapeDtypeStruct((chips, 3 * hidden, lanes), jnp.bfloat16)
    other, pre, activation, flat = pl.pallas_call(
        functools.partial(passes_kernel, width),
        out_shape=(
            grads_shape,
            jax.ShapeDtypeStruct((2 * hidden, rows), jnp.bfloat16),
            jax.ShapeDtypeStruct((hidden, rows), jnp.bfloat16),
            jax.ShapeDtypeStruct((2, rows, flat_lanes), jnp.bfloat16),
        ),
        in_specs=[smem, smem] + [vmem] * 8,
        out_specs=(vmem,) * 4,
        scratch_shapes=[
            pltpu.VMEM((2, hidden, rows), jnp.float32),
            pltpu.VMEM((hidden, rows), jnp.float32),
        ],
        compiler_params=pltpu.CompilerParams(vmem_limit_bytes=12 * 2**20),
    )(replica, piece_at, first, low, high, w_gate, up_here, down_here, forward, back)
    swap = [(i, i ^ 1) for i in range(replicas)]
    theirs = lax.ppermute(other, "dp", swap)
    mine = pl.pallas_call(
        functools.partial(own_kernel, width),
        out_shape=grads_shape,
        in_specs=[smem] + [vmem] * 3,
        out_specs=vmem,
        compiler_params=pltpu.CompilerParams(vmem_limit_bytes=12 * 2**20),
        cost_estimate=pl.CostEstimate(
            flops=6 * hidden * rows * feature_count, bytes_accessed=4 * 2**20, transcendentals=0
        ),
    )(replica, pre, activation, flat)
    chunk_shape = jax.ShapeDtypeStruct((3 * hidden, lanes), jnp.bfloat16)
    small = pltpu.CompilerParams(vmem_limit_bytes=12 * 2**20)
    chunks = pl.pallas_call(
        chip_kernel,
        out_shape=(chunk_shape,) * chips,
        in_specs=[smem, vmem, vmem],
        out_specs=(vmem,) * chips,
        compiler_params=small,
    )(replica, mine, theirs)
    add = pl.pallas_call(
        add_kernel,
        out_shape=chunk_shape,
        in_specs=[vmem, vmem],
        out_specs=vmem,
        compiler_params=small,
    )
    far = chips // 2
    chunks = list(chunks)
    piece_grad = pl.pallas_call(
        piece_kernel,
        out_shape=pltpu.HBM((device_count, CAP, feature_count), jnp.bfloat16),
        in_specs=[vmem] * 3,
        out_specs=hbm,
        scratch_shapes=[
            pltpu.VMEM((device_count, CAP, feature_count), jnp.bfloat16),
            pltpu.SemaphoreType.DMA(()),
        ],
        compiler_params=pltpu.CompilerParams(vmem_limit_bytes=12 * 2**20),
        cost_estimate=pl.CostEstimate(
            flops=4 * hidden * rows * feature_count, bytes_accessed=4 * 2**20, transcendentals=0
        ),
    )(pre, w_gate, up_here)
    chunks[far], piece_grad = lax.optimization_barrier((chunks[far], piece_grad))
    ahead = [(i, (i + 2) % replicas) for i in range(replicas)]
    back = [(i, (i - 2) % replicas) for i in range(replicas)]
    rising = lax.ppermute(chunks[far], "dp", ahead)
    falling = lax.ppermute(chunks[chips - far + 1], "dp", back)
    for distance in range(far - 1, 0, -1):
        rising = lax.ppermute(add(rising, chunks[distance]), "dp", ahead)
        if distance > 1:
            falling = lax.ppermute(add(falling, chunks[chips - distance + 1]), "dp", back)
    returned = lax.all_to_all(piece_grad, "expert", split_axis=0, concat_axis=0, tiled=True)
    grad_tokens = pl.pallas_call(
        combine_kernel,
        out_shape=jax.ShapeDtypeStruct((token_count, feature_count), jnp.bfloat16),
        in_specs=[vmem, vmem],
        out_specs=vmem,
        compiler_params=small,
        cost_estimate=pl.CostEstimate(
            flops=2 * rows * token_count * feature_count,
            bytes_accessed=2 * 2**20,
            transcendentals=0,
        ),
    )(table, returned)
    falling, grad_tokens = lax.optimization_barrier((falling, grad_tokens))
    owned = jax.ShapeDtypeStruct((hidden, width), jnp.bfloat16)
    grads = pl.pallas_call(
        total_kernel,
        out_shape=(owned,) * 3,
        in_specs=[vmem] * 3,
        out_specs=(vmem,) * 3,
        compiler_params=small,
    )(rising, falling, chunks[0])
    return (grad_tokens, *grads)


def solution(mesh):
    in_specs = (
        P(("expert", "dp"), None),
        P(("expert", "dp"), None),
        P(("expert", "dp"), None),
        P(("expert", "dp"), None),
        P("expert", None),
        P("expert", None),
        P("expert", None),
    )
    out_specs = (P(("expert", "dp"), None), P("expert", "dp"), P("expert", "dp"), P("expert", "dp"))
    return jax.shard_map(shards, mesh=mesh, in_specs=in_specs, out_specs=out_specs, check_vma=False)
```

```python
import functools

import jax
import jax.numpy as jnp
from jax import lax
from jax.experimental import pallas as pl
from jax.experimental.pallas import tpu as pltpu
from jax.sharding import PartitionSpec as P

EXPERTS = 4
CAP = 2
LOADS = 4


def select_kernel(
    ids_hbm, gates_hbm, tokens_hbm, cotan_hbm, send_ref, table_ref, ids_ref, gates_ref, tokens_ref,
    cotan_ref, rows_ref, in_sems, row_sems, out_sems,
):
    slots, tokens = EXPERTS * CAP, table_ref.shape[1]
    load_ids = pltpu.make_async_copy(ids_hbm, ids_ref, in_sems.at[0])
    load_gates = pltpu.make_async_copy(gates_hbm, gates_ref, in_sems.at[1])
    load_ids.start()
    load_gates.start()
    tall = tokens_ref.shape[0] // LOADS
    loads = [
        [
            pltpu.make_async_copy(
                source.at[pl.ds(part * tall, tall)],
                target.at[pl.ds(part * tall, tall)],
                row_sems.at[index, part],
            )
            for part in range(LOADS)
        ]
        for index, (source, target) in enumerate(
            ((tokens_hbm, tokens_ref), (cotan_hbm, cotan_ref))
        )
    ]
    for part in loads[0] + loads[1]:
        part.start()
    slot = lax.broadcasted_iota(jnp.int32, (slots, tokens), 0)
    expert, place = slot // CAP, slot % CAP
    earlier = lax.broadcasted_iota(jnp.int32, (tokens, tokens), 0) < lax.broadcasted_iota(
        jnp.int32, (tokens, tokens), 1
    )
    earlier = jnp.where(earlier, 1.0, 0.0).astype(jnp.bfloat16)
    load_ids.wait()
    first = ids_ref[0:1, :] == expert
    second = ids_ref[1:2, :] == expert
    named = jnp.where(first | second, 1.0, 0.0)
    before = jnp.dot(named.astype(jnp.bfloat16), earlier, preferred_element_type=jnp.float32)
    table = jnp.where(before == place.astype(jnp.float32), named, 0.0)
    sub = lax.broadcasted_iota(jnp.int32, table_ref.shape, 0)
    per_expert = table_ref.shape[0] // EXPERTS
    repeated = jnp.zeros(table_ref.shape, jnp.float32)
    for e in range(EXPERTS):
        for p in range(CAP):
            here = (sub // per_expert == e) & (sub % CAP == p)
            repeated = jnp.where(here, table[e * CAP + p : e * CAP + p + 1, :], repeated)
    table_ref[...] = repeated.astype(jnp.bfloat16)
    load_gates.wait()
    gates = gates_ref[...].astype(jnp.float32)
    gated = table * jnp.where(first, gates[0:1, :], gates[1:2, :])
    stores = []
    for half, (weight, source_ref) in enumerate(((table, tokens_ref), (gated, cotan_ref))):
        for part in loads[half]:
            part.wait()
        picked = jnp.dot(
            weight.astype(jnp.bfloat16), source_ref[...], preferred_element_type=jnp.float32
        )
        for e in range(EXPERTS):
            rows_ref[half, e] = picked[e * CAP : (e + 1) * CAP].astype(jnp.bfloat16)
        for piece in range(half, send_ref.shape[1], 2):
            store = pltpu.make_async_copy(
                rows_ref.at[half], send_ref.at[:, piece], out_sems.at[piece]
            )
            store.start()
            stores.append(store)
    for store in stores:
        store.wait()


def chunk_grads(width, core, pre, activation, inputs, cotan, out_ref):
    chunks, _, lanes = out_ref.shape
    for chunk in range(chunks):
        start = (chunk * 2 + core) * width
        part = jnp.concatenate(
            [
                jnp.dot(pre, inputs[:, start : start + lanes], preferred_element_type=jnp.float32),
                jnp.dot(
                    activation, cotan[:, start : start + lanes], preferred_element_type=jnp.float32
                ),
            ],
            axis=0,
        )
        out_ref[chunk] = part.astype(jnp.bfloat16)


def part_kernel(start, rows_ref, part_ref):
    part_ref[...] = rows_ref[start : start + part_ref.shape[0]]


def flatten(rows_ref, lanes):
    sources, cap, features = rows_ref.shape
    flat = rows_ref[...].reshape(sources * cap, features)
    beyond = jnp.zeros((sources * cap, lanes - features), jnp.bfloat16)
    return jnp.concatenate([flat, beyond], axis=1)


def project(weight_ref, rows):
    across = (((1,), (1,)), ((), ()))
    features = weight_ref.shape[1]
    return lax.dot_general(
        weight_ref[...], rows[:, :features], across, preferred_element_type=jnp.float32
    )


def first_kernel(
    piece_at_ref, rows_ref, gate_ref, up_hbm, down_hbm, flat_ref, up_ref, down_ref, forward_ref, back_ref,
    sems,
):
    load_up = pltpu.make_async_copy(up_hbm, up_ref, sems.at[0])
    load_down = pltpu.make_async_copy(down_hbm, down_ref, sems.at[1])
    load_up.start()
    load_down.start()
    flat_ref[...] = flatten(rows_ref, flat_ref.shape[1])

    @pl.when(piece_at_ref[0] & 1 == 0)
    def _():
        forward_ref[0] = project(gate_ref, flat_ref)

    load_up.wait()
    load_down.wait()

    @pl.when(piece_at_ref[0] & 1 == 0)
    def _():
        forward_ref[1] = project(up_ref, flat_ref)

    @pl.when(piece_at_ref[0] & 1 == 1)
    def _():
        back_ref[...] = project(down_ref, flat_ref)


def passes_kernel(
    width, replica_ref, piece_at_ref, first_ref, low_ref, high_ref, gate_ref, up_ref, down_ref, done_forward_ref,
    done_back_ref, other_ref, pre_ref, act_ref, flat_ref, forward_ref, back_ref,
):
    half = CAP * low_ref.shape[0]
    odd = piece_at_ref[0] & 1
    flat_ref[odd] = first_ref[...]
    flat_ref[1 - odd, :half] = flatten(low_ref, flat_ref.shape[2])
    flat_ref[1 - odd, half:] = flatten(high_ref, flat_ref.shape[2])

    @pl.when(odd == 0)
    def _():
        forward_ref[...] = done_forward_ref[...]
        back_ref[...] = project(down_ref, flat_ref.at[1])

    @pl.when(odd == 1)
    def _():
        forward_ref[0] = project(gate_ref, flat_ref.at[0])
        forward_ref[1] = project(up_ref, flat_ref.at[0])
        back_ref[...] = done_back_ref[...]

    gate_pre, up_pre, hidden = forward_ref[0], forward_ref[1], back_ref[...]
    sig = 1.0 / (1.0 + jnp.exp(-gate_pre))
    activation = (gate_pre * sig * up_pre).astype(jnp.bfloat16)
    grad_up = hidden * gate_pre * sig
    grad_gate = hidden * up_pre * sig * (1.0 + gate_pre * (1.0 - sig))
    pre = jnp.concatenate([grad_gate, grad_up], axis=0).astype(jnp.bfloat16)
    pre_ref[...] = pre
    act_ref[...] = activation
    for core in range(2):

        @pl.when(replica_ref[0] & 1 == core)
        def _():
            chunk_grads(width, 1 - core, pre, activation, flat_ref[0], flat_ref[1], other_ref)


def own_kernel(width, replica_ref, pre_ref, act_ref, flat_ref, mine_ref):
    for core in range(2):

        @pl.when(replica_ref[0] & 1 == core)
        def _():
            chunk_grads(width, core, pre_ref[...], act_ref[...], flat_ref[0], flat_ref[1], mine_ref)


def piece_kernel(pre_ref, gate_ref, up_ref, piece_hbm, piece_ref, sem):
    hidden = gate_ref.shape[0]
    pre = pre_ref[...].astype(jnp.float32)
    down = (((0,), (0,)), ((), ()))
    piece = lax.dot_general(
        pre[:hidden].astype(jnp.bfloat16), gate_ref[...], down, preferred_element_type=jnp.float32
    ) + lax.dot_general(
        pre[hidden:].astype(jnp.bfloat16), up_ref[...], down, preferred_element_type=jnp.float32
    )
    piece_ref[...] = piece.astype(jnp.bfloat16).reshape(piece_ref.shape)
    store = pltpu.make_async_copy(piece_ref, piece_hbm, sem)
    store.start()
    store.wait()


def combine_kernel(table_ref, rows_ref, tokens_ref):
    flat = rows_ref[...].reshape(table_ref.shape[0], tokens_ref.shape[1])
    total = lax.dot_general(
        table_ref[...], flat, (((0,), (0,)), ((), ())), preferred_element_type=jnp.float32
    )
    tokens_ref[...] = total.astype(jnp.bfloat16)


def added(first, second):
    return (first.astype(jnp.float32) + second.astype(jnp.float32)).astype(jnp.bfloat16)


def chip_kernel(replica_ref, mine_ref, theirs_ref, *out_refs):
    chips = len(out_refs)
    for distance, out_ref in enumerate(out_refs):
        chunk = ((replica_ref[0] >> 1) + distance) & (chips - 1)
        out_ref[...] = added(mine_ref[chunk], theirs_ref[chunk])


def add_kernel(got_ref, own_ref, sum_ref):
    sum_ref[...] = added(got_ref[...], own_ref[...])


def total_kernel(up_ring_ref, down_ring_ref, own_ref, gate_ref, up_ref, down_ref):
    hidden, width = gate_ref.shape
    total = up_ring_ref[...].astype(jnp.float32) + down_ring_ref[...].astype(jnp.float32)
    total = total + own_ref[...].astype(jnp.float32)
    for index, out_ref in enumerate((gate_ref, up_ref, down_ref)):
        rows = total[index * hidden : (index + 1) * hidden]
        out_ref[...] = rows[:, :width].astype(jnp.bfloat16)


def shards(tokens, cotangent, gates, route_ids, w_gate, w_up, w_down):
    device_count = lax.axis_size("expert")
    replicas = lax.axis_size("dp")
    pieces = device_count // EXPERTS
    token_count, feature_count = tokens.shape
    hidden = w_gate.shape[0]
    chips = replicas // 2
    width = feature_count // replicas
    lanes = -(-width // 128) * 128
    rows = device_count * CAP
    vmem = pl.BlockSpec(memory_space=pltpu.VMEM)
    smem = pl.BlockSpec(memory_space=pltpu.SMEM)
    hbm = pl.BlockSpec(memory_space=pltpu.HBM)
    in_hbm = functools.partial(pltpu.with_memory_space_constraint, memory_space=pltpu.HBM)
    send, table = pl.pallas_call(
        select_kernel,
        out_shape=(
            pltpu.HBM((EXPERTS, pieces, CAP, feature_count), jnp.bfloat16),
            jax.ShapeDtypeStruct((rows, token_count), jnp.bfloat16),
        ),
        in_specs=[hbm] * 4,
        out_specs=(hbm, vmem),
        scratch_shapes=[
            pltpu.VMEM((2, token_count), jnp.int32),
            pltpu.VMEM((2, token_count), jnp.bfloat16),
            pltpu.VMEM((token_count, feature_count), jnp.bfloat16),
            pltpu.VMEM((token_count, feature_count), jnp.bfloat16),
            pltpu.VMEM((2, EXPERTS, CAP, feature_count), jnp.bfloat16),
            pltpu.SemaphoreType.DMA((2,)),
            pltpu.SemaphoreType.DMA((2, LOADS)),
            pltpu.SemaphoreType.DMA((pieces,)),
        ],
        compiler_params=pltpu.CompilerParams(vmem_limit_bytes=16 * 2**20),
    )(in_hbm(route_ids.T), in_hbm(gates.T), in_hbm(tokens), in_hbm(cotangent))
    arrived = lax.all_to_all(
        send.reshape(device_count, CAP, feature_count),
        "expert",
        split_axis=0,
        concat_axis=0,
        tiled=True,
    )
    ring = pieces // 2
    after = [(i, i // ring * ring + (i + 1) % ring) for i in range(device_count)]
    before = [(i, i // ring * ring + (i - 1) % ring) for i in range(device_count)]
    split = device_count // 2

    def part(start, size):
        return pl.pallas_call(
            functools.partial(part_kernel, start),
            out_shape=jax.ShapeDtypeStruct((size, CAP, feature_count), jnp.bfloat16),
            in_specs=[vmem],
            out_specs=vmem,
            compiler_params=pltpu.CompilerParams(vmem_limit_bytes=12 * 2**20),
        )(arrived)

    low, high = part(0, split), part(split, device_count - split)
    low = lax.ppermute(low, "expert", after)
    high = lax.ppermute(high, "expert", before)
    piece_at = lax.axis_index("expert").astype(jnp.int32).reshape(1)
    replica = lax.axis_index("dp").astype(jnp.int32).reshape(1)
    flat_lanes = feature_count + lanes // 2
    weight_shape = jax.ShapeDtypeStruct((hidden, feature_count), jnp.bfloat16)
    forward_shape = jax.ShapeDtypeStruct((2, hidden, rows), jnp.float32)
    back_shape = jax.ShapeDtypeStruct((hidden, rows), jnp.float32)
    first, up_here, down_here, forward, back = pl.pallas_call(
        first_kernel,
        out_shape=(
            jax.ShapeDtypeStruct((rows, flat_lanes), jnp.bfloat16),
            weight_shape,
            weight_shape,
            forward_shape,
            back_shape,
        ),
        in_specs=[smem, vmem, vmem, hbm, hbm],
        out_specs=(vmem,) * 5,
        scratch_shapes=[pltpu.SemaphoreType.DMA((2,))],
        compiler_params=pltpu.CompilerParams(vmem_limit_bytes=12 * 2**20),
        cost_estimate=pl.CostEstimate(
            flops=4 * hidden * rows * feature_count, bytes_accessed=8 * 2**20, transcendentals=0
        ),
    )(piece_at, arrived, w_gate, in_hbm(w_up), in_hbm(w_down))
    grads_shape = jax.ShapeDtypeStruct((chips, 3 * hidden, lanes), jnp.bfloat16)
    other, pre, activation, flat = pl.pallas_call(
        functools.partial(passes_kernel, width),
        out_shape=(
            grads_shape,
            jax.ShapeDtypeStruct((2 * hidden, rows), jnp.bfloat16),
            jax.ShapeDtypeStruct((hidden, rows), jnp.bfloat16),
            jax.ShapeDtypeStruct((2, rows, flat_lanes), jnp.bfloat16),
        ),
        in_specs=[smem, smem] + [vmem] * 8,
        out_specs=(vmem,) * 4,
        scratch_shapes=[
            pltpu.VMEM((2, hidden, rows), jnp.float32),
            pltpu.VMEM((hidden, rows), jnp.float32),
        ],
        compiler_params=pltpu.CompilerParams(vmem_limit_bytes=12 * 2**20),
    )(replica, piece_at, first, low, high, w_gate, up_here, down_here, forward, back)
    swap = [(i, i ^ 1) for i in range(replicas)]
    theirs = lax.ppermute(other, "dp", swap)
    mine = pl.pallas_call(
        functools.partial(own_kernel, width),
        out_shape=grads_shape,
        in_specs=[smem] + [vmem] * 3,
        out_specs=vmem,
        compiler_params=pltpu.CompilerParams(vmem_limit_bytes=12 * 2**20),
        cost_estimate=pl.CostEstimate(
            flops=6 * hidden * rows * feature_count, bytes_accessed=4 * 2**20, transcendentals=0
        ),
    )(replica, pre, activation, flat)
    chunk_shape = jax.ShapeDtypeStruct((3 * hidden, lanes), jnp.bfloat16)
    small = pltpu.CompilerParams(vmem_limit_bytes=12 * 2**20)
    chunks = pl.pallas_call(
        chip_kernel,
        out_shape=(chunk_shape,) * chips,
        in_specs=[smem, vmem, vmem],
        out_specs=(vmem,) * chips,
        compiler_params=small,
    )(replica, mine, theirs)
    add = pl.pallas_call(
        add_kernel,
        out_shape=chunk_shape,
        in_specs=[vmem, vmem],
        out_specs=vmem,
        compiler_params=small,
    )
    far = chips // 2
    chunks = list(chunks)
    piece_grad = pl.pallas_call(
        piece_kernel,
        out_shape=pltpu.HBM((device_count, CAP, feature_count), jnp.bfloat16),
        in_specs=[vmem] * 3,
        out_specs=hbm,
        scratch_shapes=[
            pltpu.VMEM((device_count, CAP, feature_count), jnp.bfloat16),
            pltpu.SemaphoreType.DMA(()),
        ],
        compiler_params=pltpu.CompilerParams(vmem_limit_bytes=12 * 2**20),
        cost_estimate=pl.CostEstimate(
            flops=4 * hidden * rows * feature_count, bytes_accessed=4 * 2**20, transcendentals=0
        ),
    )(pre, w_gate, up_here)
    chunks[far], piece_grad = lax.optimization_barrier((chunks[far], piece_grad))
    ahead = [(i, (i + 2) % replicas) for i in range(replicas)]
    back = [(i, (i - 2) % replicas) for i in range(replicas)]
    rising = lax.ppermute(chunks[far], "dp", ahead)
    falling = lax.ppermute(chunks[chips - far + 1], "dp", back)
    for distance in range(far - 1, 0, -1):
        rising = lax.ppermute(add(rising, chunks[distance]), "dp", ahead)
        if distance > 1:
            falling = lax.ppermute(add(falling, chunks[chips - distance + 1]), "dp", back)
    returned = lax.all_to_all(piece_grad, "expert", split_axis=0, concat_axis=0, tiled=True)
    grad_tokens = pl.pallas_call(
        combine_kernel,
        out_shape=jax.ShapeDtypeStruct((token_count, feature_count), jnp.bfloat16),
        in_specs=[vmem, vmem],
        out_specs=vmem,
        compiler_params=small,
        cost_estimate=pl.CostEstimate(
            flops=2 * rows * token_count * feature_count,
            bytes_accessed=2 * 2**20,
            transcendentals=0,
        ),
    )(table, returned)
    falling, grad_tokens = lax.optimization_barrier((falling, grad_tokens))
    owned = jax.ShapeDtypeStruct((hidden, width), jnp.bfloat16)
    grads = pl.pallas_call(
        total_kernel,
        out_shape=(owned,) * 3,
        in_specs=[vmem] * 3,
        out_specs=(vmem,) * 3,
        compiler_params=small,
    )(rising, falling, chunks[0])
    return (grad_tokens, *grads)


def solution(mesh):
    in_specs = (
        P(("expert", "dp"), None),
        P(("expert", "dp"), None),
        P(("expert", "dp"), None),
        P(("expert", "dp"), None),
        P("expert", None),
        P("expert", None),
        P("expert", None),
    )
    out_specs = (P(("expert", "dp"), None), P("expert", "dp"), P("expert", "dp"), P("expert", "dp"))
    return jax.shard_map(shards, mesh=mesh, in_specs=in_specs, out_specs=out_specs, check_vma=False)
```

```python
import functools

import jax
import jax.numpy as jnp
from jax import lax
from jax.experimental import pallas as pl
from jax.experimental.pallas import tpu as pltpu
from jax.sharding import PartitionSpec as P

EXPERTS = 4
CAP = 2


def select_kernel(
    ids_hbm, gates_hbm, tokens_hbm, cotan_hbm, send_ref, table_ref, ids_ref, gates_ref, tokens_ref,
    cotan_ref, rows_ref, in_sems, out_sems,
):
    slots, tokens = EXPERTS * CAP, table_ref.shape[1]
    loads = [
        pltpu.make_async_copy(source, target, in_sems.at[index])
        for index, (source, target) in enumerate(
            (
                (ids_hbm, ids_ref),
                (gates_hbm, gates_ref),
                (tokens_hbm, tokens_ref),
                (cotan_hbm, cotan_ref),
            )
        )
    ]
    for load in loads:
        load.start()
    slot = lax.broadcasted_iota(jnp.int32, (slots, tokens), 0)
    expert, place = slot // CAP, slot % CAP
    earlier = lax.broadcasted_iota(jnp.int32, (tokens, tokens), 0) < lax.broadcasted_iota(
        jnp.int32, (tokens, tokens), 1
    )
    earlier = jnp.where(earlier, 1.0, 0.0).astype(jnp.bfloat16)
    loads[0].wait()
    first = ids_ref[0:1, :] == expert
    second = ids_ref[1:2, :] == expert
    named = jnp.where(first | second, 1.0, 0.0)
    before = jnp.dot(named.astype(jnp.bfloat16), earlier, preferred_element_type=jnp.float32)
    table = jnp.where(before == place.astype(jnp.float32), named, 0.0)
    sub = lax.broadcasted_iota(jnp.int32, table_ref.shape, 0)
    per_expert = table_ref.shape[0] // EXPERTS
    repeated = jnp.zeros(table_ref.shape, jnp.float32)
    for e in range(EXPERTS):
        for p in range(CAP):
            here = (sub // per_expert == e) & (sub % CAP == p)
            repeated = jnp.where(here, table[e * CAP + p : e * CAP + p + 1, :], repeated)
    table_ref[...] = repeated.astype(jnp.bfloat16)
    loads[1].wait()
    gates = gates_ref[...].astype(jnp.float32)
    gated = table * jnp.where(first, gates[0:1, :], gates[1:2, :])
    stores = []
    for half, (weight, source_ref) in enumerate(((table, tokens_ref), (gated, cotan_ref))):
        loads[2 + half].wait()
        picked = jnp.dot(
            weight.astype(jnp.bfloat16), source_ref[...], preferred_element_type=jnp.float32
        )
        for e in range(EXPERTS):
            rows_ref[half, e] = picked[e * CAP : (e + 1) * CAP].astype(jnp.bfloat16)
        for piece in range(half, send_ref.shape[1], 2):
            store = pltpu.make_async_copy(
                rows_ref.at[half], send_ref.at[:, piece], out_sems.at[piece]
            )
            store.start()
            stores.append(store)
    for store in stores:
        store.wait()


def chunk_grads(width, core, pre, activation, inputs, cotan, out_ref):
    chunks, _, lanes = out_ref.shape
    for chunk in range(chunks):
        start = (chunk * 2 + core) * width
        part = jnp.concatenate(
            [
                jnp.dot(pre, inputs[:, start : start + lanes], preferred_element_type=jnp.float32),
                jnp.dot(
                    activation, cotan[:, start : start + lanes], preferred_element_type=jnp.float32
                ),
            ],
            axis=0,
        )
        out_ref[chunk] = part.astype(jnp.bfloat16)


def part_kernel(start, rows_ref, part_ref):
    part_ref[...] = rows_ref[start : start + part_ref.shape[0]]


def flatten(rows, lanes):
    sources, cap, features = rows.shape
    flat = rows.reshape(sources * cap, features)
    beyond = jnp.zeros((sources * cap, lanes - features), jnp.bfloat16)
    return jnp.concatenate([flat, beyond], axis=1)


def project(weight_ref, rows):
    across = (((1,), (1,)), ((), ()))
    features = weight_ref.shape[1]
    return lax.dot_general(
        weight_ref[...], rows[:, :features], across, preferred_element_type=jnp.float32
    )


def first_kernel(
    piece_at_ref, rows_ref, gate_ref, up_hbm, down_hbm, flat_ref, up_ref, down_ref, forward_ref, back_ref,
    sems,
):
    load_up = pltpu.make_async_copy(up_hbm, up_ref, sems.at[0])
    load_down = pltpu.make_async_copy(down_hbm, down_ref, sems.at[1])
    load_up.start()
    load_down.start()
    flat_ref[...] = flatten(rows_ref[...], flat_ref.shape[1])

    @pl.when(piece_at_ref[0] & 1 == 0)
    def _():
        forward_ref[0] = project(gate_ref, flat_ref)

    load_up.wait()
    load_down.wait()

    @pl.when(piece_at_ref[0] & 1 == 0)
    def _():
        forward_ref[1] = project(up_ref, flat_ref)

    @pl.when(piece_at_ref[0] & 1 == 1)
    def _():
        back_ref[...] = project(down_ref, flat_ref)


def passes_kernel(
    width, replica_ref, piece_at_ref, first_ref, low_ref, high_ref, gate_ref, up_ref, down_ref, done_forward_ref,
    done_back_ref, other_ref, pre_ref, act_ref, flat_ref, forward_ref, back_ref,
):
    odd = piece_at_ref[0] & 1
    flat_ref[odd] = first_ref[...]
    traded = jnp.concatenate([low_ref[...], high_ref[...]], axis=0)
    flat_ref[1 - odd] = flatten(traded, flat_ref.shape[2])

    @pl.when(odd == 0)
    def _():
        forward_ref[...] = done_forward_ref[...]
        back_ref[...] = project(down_ref, flat_ref.at[1])

    @pl.when(odd == 1)
    def _():
        forward_ref[0] = project(gate_ref, flat_ref.at[0])
        forward_ref[1] = project(up_ref, flat_ref.at[0])
        back_ref[...] = done_back_ref[...]

    gate_pre, up_pre, hidden = forward_ref[0], forward_ref[1], back_ref[...]
    sig = 1.0 / (1.0 + jnp.exp(-gate_pre))
    activation = (gate_pre * sig * up_pre).astype(jnp.bfloat16)
    grad_up = hidden * gate_pre * sig
    grad_gate = hidden * up_pre * sig * (1.0 + gate_pre * (1.0 - sig))
    pre = jnp.concatenate([grad_gate, grad_up], axis=0).astype(jnp.bfloat16)
    pre_ref[...] = pre
    act_ref[...] = activation
    for core in range(2):

        @pl.when(replica_ref[0] & 1 == core)
        def _():
            chunk_grads(width, 1 - core, pre, activation, flat_ref[0], flat_ref[1], other_ref)


def own_kernel(width, replica_ref, pre_ref, act_ref, flat_ref, mine_ref):
    for core in range(2):

        @pl.when(replica_ref[0] & 1 == core)
        def _():
            chunk_grads(width, core, pre_ref[...], act_ref[...], flat_ref[0], flat_ref[1], mine_ref)


def piece_kernel(pre_ref, gate_ref, up_ref, piece_hbm, piece_ref, sem):
    hidden = gate_ref.shape[0]
    pre = pre_ref[...].astype(jnp.float32)
    down = (((0,), (0,)), ((), ()))
    piece = lax.dot_general(
        pre[:hidden].astype(jnp.bfloat16), gate_ref[...], down, preferred_element_type=jnp.float32
    ) + lax.dot_general(
        pre[hidden:].astype(jnp.bfloat16), up_ref[...], down, preferred_element_type=jnp.float32
    )
    piece_ref[...] = piece.astype(jnp.bfloat16).reshape(piece_ref.shape)
    store = pltpu.make_async_copy(piece_ref, piece_hbm, sem)
    store.start()
    store.wait()


def combine_kernel(table_ref, rows_ref, tokens_ref):
    flat = rows_ref[...].reshape(table_ref.shape[0], tokens_ref.shape[1])
    total = lax.dot_general(
        table_ref[...], flat, (((0,), (0,)), ((), ())), preferred_element_type=jnp.float32
    )
    tokens_ref[...] = total.astype(jnp.bfloat16)


def added(first, second):
    return (first.astype(jnp.float32) + second.astype(jnp.float32)).astype(jnp.bfloat16)


def chip_kernel(replica_ref, mine_ref, theirs_ref, *out_refs):
    chips = len(out_refs)
    for distance, out_ref in enumerate(out_refs):
        chunk = ((replica_ref[0] >> 1) + distance) & (chips - 1)
        out_ref[...] = added(mine_ref[chunk], theirs_ref[chunk])


def add_kernel(got_ref, own_ref, sum_ref):
    sum_ref[...] = added(got_ref[...], own_ref[...])


def total_kernel(up_ring_ref, down_ring_ref, own_ref, gate_ref, up_ref, down_ref):
    hidden, width = gate_ref.shape
    total = up_ring_ref[...].astype(jnp.float32) + down_ring_ref[...].astype(jnp.float32)
    total = total + own_ref[...].astype(jnp.float32)
    for index, out_ref in enumerate((gate_ref, up_ref, down_ref)):
        rows = total[index * hidden : (index + 1) * hidden]
        out_ref[...] = rows[:, :width].astype(jnp.bfloat16)


def shards(tokens, cotangent, gates, route_ids, w_gate, w_up, w_down):
    device_count = lax.axis_size("expert")
    replicas = lax.axis_size("dp")
    pieces = device_count // EXPERTS
    token_count, feature_count = tokens.shape
    hidden = w_gate.shape[0]
    chips = replicas // 2
    width = feature_count // replicas
    lanes = -(-width // 128) * 128
    rows = device_count * CAP
    vmem = pl.BlockSpec(memory_space=pltpu.VMEM)
    smem = pl.BlockSpec(memory_space=pltpu.SMEM)
    hbm = pl.BlockSpec(memory_space=pltpu.HBM)
    in_hbm = functools.partial(pltpu.with_memory_space_constraint, memory_space=pltpu.HBM)
    send, table = pl.pallas_call(
        select_kernel,
        out_shape=(
            pltpu.HBM((EXPERTS, pieces, CAP, feature_count), jnp.bfloat16),
            jax.ShapeDtypeStruct((rows, token_count), jnp.bfloat16),
        ),
        in_specs=[hbm] * 4,
        out_specs=(hbm, vmem),
        scratch_shapes=[
            pltpu.VMEM((2, token_count), jnp.int32),
            pltpu.VMEM((2, token_count), jnp.bfloat16),
            pltpu.VMEM((token_count, feature_count), jnp.bfloat16),
            pltpu.VMEM((token_count, feature_count), jnp.bfloat16),
            pltpu.VMEM((2, EXPERTS, CAP, feature_count), jnp.bfloat16),
            pltpu.SemaphoreType.DMA((4,)),
            pltpu.SemaphoreType.DMA((pieces,)),
        ],
        compiler_params=pltpu.CompilerParams(vmem_limit_bytes=16 * 2**20),
    )(in_hbm(route_ids.T), in_hbm(gates.T), in_hbm(tokens), in_hbm(cotangent))
    arrived = lax.all_to_all(
        send.reshape(device_count, CAP, feature_count),
        "expert",
        split_axis=0,
        concat_axis=0,
        tiled=True,
    )
    ring = pieces // 2
    after = [(i, i // ring * ring + (i + 1) % ring) for i in range(device_count)]
    before = [(i, i // ring * ring + (i - 1) % ring) for i in range(device_count)]
    split = device_count * 5 // 8

    def part(start, size):
        return pl.pallas_call(
            functools.partial(part_kernel, start),
            out_shape=jax.ShapeDtypeStruct((size, CAP, feature_count), jnp.bfloat16),
            in_specs=[vmem],
            out_specs=vmem,
            compiler_params=pltpu.CompilerParams(vmem_limit_bytes=12 * 2**20),
        )(arrived)

    low, high = part(0, split), part(split, device_count - split)
    low = lax.ppermute(low, "expert", after)
    high = lax.ppermute(high, "expert", before)
    piece_at = lax.axis_index("expert").astype(jnp.int32).reshape(1)
    replica = lax.axis_index("dp").astype(jnp.int32).reshape(1)
    flat_lanes = feature_count + lanes // 2
    weight_shape = jax.ShapeDtypeStruct((hidden, feature_count), jnp.bfloat16)
    forward_shape = jax.ShapeDtypeStruct((2, hidden, rows), jnp.float32)
    back_shape = jax.ShapeDtypeStruct((hidden, rows), jnp.float32)
    first, up_here, down_here, forward, back = pl.pallas_call(
        first_kernel,
        out_shape=(
            jax.ShapeDtypeStruct((rows, flat_lanes), jnp.bfloat16),
            weight_shape,
            weight_shape,
            forward_shape,
            back_shape,
        ),
        in_specs=[smem, vmem, vmem, hbm, hbm],
        out_specs=(vmem,) * 5,
        scratch_shapes=[pltpu.SemaphoreType.DMA((2,))],
        compiler_params=pltpu.CompilerParams(vmem_limit_bytes=12 * 2**20),
        cost_estimate=pl.CostEstimate(
            flops=4 * hidden * rows * feature_count, bytes_accessed=8 * 2**20, transcendentals=0
        ),
    )(piece_at, arrived, w_gate, in_hbm(w_up), in_hbm(w_down))
    grads_shape = jax.ShapeDtypeStruct((chips, 3 * hidden, lanes), jnp.bfloat16)
    other, pre, activation, flat = pl.pallas_call(
        functools.partial(passes_kernel, width),
        out_shape=(
            grads_shape,
            jax.ShapeDtypeStruct((2 * hidden, rows), jnp.bfloat16),
            jax.ShapeDtypeStruct((hidden, rows), jnp.bfloat16),
            jax.ShapeDtypeStruct((2, rows, flat_lanes), jnp.bfloat16),
        ),
        in_specs=[smem, smem] + [vmem] * 8,
        out_specs=(vmem,) * 4,
        scratch_shapes=[
            pltpu.VMEM((2, hidden, rows), jnp.float32),
            pltpu.VMEM((hidden, rows), jnp.float32),
        ],
        compiler_params=pltpu.CompilerParams(vmem_limit_bytes=12 * 2**20),
    )(replica, piece_at, first, low, high, w_gate, up_here, down_here, forward, back)
    swap = [(i, i ^ 1) for i in range(replicas)]
    theirs = lax.ppermute(other, "dp", swap)
    mine = pl.pallas_call(
        functools.partial(own_kernel, width),
        out_shape=grads_shape,
        in_specs=[smem] + [vmem] * 3,
        out_specs=vmem,
        compiler_params=pltpu.CompilerParams(vmem_limit_bytes=12 * 2**20),
        cost_estimate=pl.CostEstimate(
            flops=6 * hidden * rows * feature_count, bytes_accessed=4 * 2**20, transcendentals=0
        ),
    )(replica, pre, activation, flat)
    chunk_shape = jax.ShapeDtypeStruct((3 * hidden, lanes), jnp.bfloat16)
    small = pltpu.CompilerParams(vmem_limit_bytes=12 * 2**20)
    chunks = pl.pallas_call(
        chip_kernel,
        out_shape=(chunk_shape,) * chips,
        in_specs=[smem, vmem, vmem],
        out_specs=(vmem,) * chips,
        compiler_params=small,
    )(replica, mine, theirs)
    add = pl.pallas_call(
        add_kernel,
        out_shape=chunk_shape,
        in_specs=[vmem, vmem],
        out_specs=vmem,
        compiler_params=small,
    )
    far = chips // 2
    chunks = list(chunks)
    piece_grad = pl.pallas_call(
        piece_kernel,
        out_shape=pltpu.HBM((device_count, CAP, feature_count), jnp.bfloat16),
        in_specs=[vmem] * 3,
        out_specs=hbm,
        scratch_shapes=[
            pltpu.VMEM((device_count, CAP, feature_count), jnp.bfloat16),
            pltpu.SemaphoreType.DMA(()),
        ],
        compiler_params=pltpu.CompilerParams(vmem_limit_bytes=12 * 2**20),
        cost_estimate=pl.CostEstimate(
            flops=4 * hidden * rows * feature_count, bytes_accessed=4 * 2**20, transcendentals=0
        ),
    )(pre, w_gate, up_here)
    chunks[far], piece_grad = lax.optimization_barrier((chunks[far], piece_grad))
    ahead = [(i, (i + 2) % replicas) for i in range(replicas)]
    back = [(i, (i - 2) % replicas) for i in range(replicas)]
    rising = lax.ppermute(chunks[far], "dp", ahead)
    falling = lax.ppermute(chunks[chips - far + 1], "dp", back)
    for distance in range(far - 1, 0, -1):
        rising = lax.ppermute(add(rising, chunks[distance]), "dp", ahead)
        if distance > 1:
            falling = lax.ppermute(add(falling, chunks[chips - distance + 1]), "dp", back)
    returned = lax.all_to_all(piece_grad, "expert", split_axis=0, concat_axis=0, tiled=True)
    grad_tokens = pl.pallas_call(
        combine_kernel,
        out_shape=jax.ShapeDtypeStruct((token_count, feature_count), jnp.bfloat16),
        in_specs=[vmem, vmem],
        out_specs=vmem,
        compiler_params=small,
        cost_estimate=pl.CostEstimate(
            flops=2 * rows * token_count * feature_count,
            bytes_accessed=2 * 2**20,
            transcendentals=0,
        ),
    )(table, returned)
    falling, grad_tokens = lax.optimization_barrier((falling, grad_tokens))
    owned = jax.ShapeDtypeStruct((hidden, width), jnp.bfloat16)
    grads = pl.pallas_call(
        total_kernel,
        out_shape=(owned,) * 3,
        in_specs=[vmem] * 3,
        out_specs=(vmem,) * 3,
        compiler_params=small,
    )(rising, falling, chunks[0])
    return (grad_tokens, *grads)


def solution(mesh):
    in_specs = (
        P(("expert", "dp"), None),
        P(("expert", "dp"), None),
        P(("expert", "dp"), None),
        P(("expert", "dp"), None),
        P("expert", None),
        P("expert", None),
        P("expert", None),
    )
    out_specs = (P(("expert", "dp"), None), P("expert", "dp"), P("expert", "dp"), P("expert", "dp"))
    return jax.shard_map(shards, mesh=mesh, in_specs=in_specs, out_specs=out_specs, check_vma=False)
```

```python
import functools

import jax
import jax.numpy as jnp
from jax import lax
from jax.experimental import pallas as pl
from jax.experimental.pallas import tpu as pltpu
from jax.sharding import PartitionSpec as P

EXPERTS = 4
CAP = 2


def select_kernel(
    ids_hbm, gates_hbm, tokens_hbm, cotan_hbm, send_ref, table_ref, ids_ref, gates_ref, tokens_ref,
    cotan_ref, rows_ref, in_sems, out_sems,
):
    slots, tokens = EXPERTS * CAP, table_ref.shape[1]
    loads = [
        pltpu.make_async_copy(source, target, in_sems.at[index])
        for index, (source, target) in enumerate(
            (
                (ids_hbm, ids_ref),
                (gates_hbm, gates_ref),
                (tokens_hbm, tokens_ref),
                (cotan_hbm, cotan_ref),
            )
        )
    ]
    for load in loads:
        load.start()
    slot = lax.broadcasted_iota(jnp.int32, (slots, tokens), 0)
    expert, place = slot // CAP, slot % CAP
    earlier = lax.broadcasted_iota(jnp.int32, (tokens, tokens), 0) < lax.broadcasted_iota(
        jnp.int32, (tokens, tokens), 1
    )
    earlier = jnp.where(earlier, 1.0, 0.0).astype(jnp.bfloat16)
    loads[0].wait()
    first = ids_ref[0:1, :] == expert
    second = ids_ref[1:2, :] == expert
    named = jnp.where(first | second, 1.0, 0.0)
    before = jnp.dot(named.astype(jnp.bfloat16), earlier, preferred_element_type=jnp.float32)
    table = jnp.where(before == place.astype(jnp.float32), named, 0.0)
    sub = lax.broadcasted_iota(jnp.int32, table_ref.shape, 0)
    per_expert = table_ref.shape[0] // EXPERTS
    repeated = jnp.zeros(table_ref.shape, jnp.float32)
    for e in range(EXPERTS):
        for p in range(CAP):
            here = (sub // per_expert == e) & (sub % CAP == p)
            repeated = jnp.where(here, table[e * CAP + p : e * CAP + p + 1, :], repeated)
    table_ref[...] = repeated.astype(jnp.bfloat16)
    loads[1].wait()
    gates = gates_ref[...].astype(jnp.float32)
    gated = table * jnp.where(first, gates[0:1, :], gates[1:2, :])
    stores = []
    for half, (weight, source_ref) in enumerate(((table, tokens_ref), (gated, cotan_ref))):
        loads[2 + half].wait()
        picked = jnp.dot(
            weight.astype(jnp.bfloat16), source_ref[...], preferred_element_type=jnp.float32
        )
        for e in range(EXPERTS):
            rows_ref[half, e] = picked[e * CAP : (e + 1) * CAP].astype(jnp.bfloat16)
        for piece in range(half, send_ref.shape[1], 2):
            store = pltpu.make_async_copy(
                rows_ref.at[half], send_ref.at[:, piece], out_sems.at[piece]
            )
            store.start()
            stores.append(store)
    for store in stores:
        store.wait()


def chunk_grads(width, core, pre, activation, inputs, cotan, out_ref):
    chunks, _, lanes = out_ref.shape
    for chunk in range(chunks):
        start = (chunk * 2 + core) * width
        part = jnp.concatenate(
            [
                jnp.dot(pre, inputs[:, start : start + lanes], preferred_element_type=jnp.float32),
                jnp.dot(
                    activation, cotan[:, start : start + lanes], preferred_element_type=jnp.float32
                ),
            ],
            axis=0,
        )
        out_ref[chunk] = part.astype(jnp.bfloat16)


def part_kernel(start, rows_ref, part_ref):
    part_ref[...] = rows_ref[start : start + part_ref.shape[0]]


def flatten(rows, lanes):
    sources, cap, features = rows.shape
    flat = rows.reshape(sources * cap, features)
    beyond = jnp.zeros((sources * cap, lanes - features), jnp.bfloat16)
    return jnp.concatenate([flat, beyond], axis=1)


def project(weight_ref, rows):
    across = (((1,), (1,)), ((), ()))
    features = weight_ref.shape[1]
    return lax.dot_general(
        weight_ref[...], rows[:, :features], across, preferred_element_type=jnp.float32
    )


def first_kernel(
    piece_at_ref, rows_ref, gate_ref, up_hbm, down_hbm, flat_ref, up_ref, down_ref, forward_ref, back_ref,
    sems,
):
    load_up = pltpu.make_async_copy(up_hbm, up_ref, sems.at[0])
    load_down = pltpu.make_async_copy(down_hbm, down_ref, sems.at[1])
    load_up.start()
    load_down.start()
    flat_ref[...] = flatten(rows_ref[...], flat_ref.shape[1])

    @pl.when(piece_at_ref[0] & 1 == 0)
    def _():
        forward_ref[0] = project(gate_ref, flat_ref)

    load_up.wait()
    load_down.wait()

    @pl.when(piece_at_ref[0] & 1 == 0)
    def _():
        forward_ref[1] = project(up_ref, flat_ref)

    @pl.when(piece_at_ref[0] & 1 == 1)
    def _():
        back_ref[...] = project(down_ref, flat_ref)


def passes_kernel(
    width, replica_ref, piece_at_ref, first_ref, low_ref, high_ref, gate_ref, up_ref, down_ref, done_forward_ref,
    done_back_ref, other_ref, pre_ref, act_ref, flat_ref, forward_ref, back_ref,
):
    odd = piece_at_ref[0] & 1
    flat_ref[odd] = first_ref[...]
    traded = jnp.concatenate([low_ref[...], high_ref[...]], axis=0)
    flat_ref[1 - odd] = flatten(traded, flat_ref.shape[2])

    @pl.when(odd == 0)
    def _():
        forward_ref[...] = done_forward_ref[...]
        back_ref[...] = project(down_ref, flat_ref.at[1])

    @pl.when(odd == 1)
    def _():
        forward_ref[0] = project(gate_ref, flat_ref.at[0])
        forward_ref[1] = project(up_ref, flat_ref.at[0])
        back_ref[...] = done_back_ref[...]

    gate_pre, up_pre, hidden = forward_ref[0], forward_ref[1], back_ref[...]
    sig = 1.0 / (1.0 + jnp.exp(-gate_pre))
    activation = (gate_pre * sig * up_pre).astype(jnp.bfloat16)
    grad_up = hidden * gate_pre * sig
    grad_gate = hidden * up_pre * sig * (1.0 + gate_pre * (1.0 - sig))
    pre = jnp.concatenate([grad_gate, grad_up], axis=0).astype(jnp.bfloat16)
    pre_ref[...] = pre
    act_ref[...] = activation
    for core in range(2):

        @pl.when(replica_ref[0] & 1 == core)
        def _():
            chunk_grads(width, 1 - core, pre, activation, flat_ref[0], flat_ref[1], other_ref)


def own_kernel(width, replica_ref, pre_ref, act_ref, flat_ref, mine_ref):
    for core in range(2):

        @pl.when(replica_ref[0] & 1 == core)
        def _():
            chunk_grads(width, core, pre_ref[...], act_ref[...], flat_ref[0], flat_ref[1], mine_ref)


def piece_kernel(pre_ref, gate_ref, up_ref, piece_hbm, piece_ref, sem):
    hidden = gate_ref.shape[0]
    pre = pre_ref[...].astype(jnp.float32)
    down = (((0,), (0,)), ((), ()))
    piece = lax.dot_general(
        pre[:hidden].astype(jnp.bfloat16), gate_ref[...], down, preferred_element_type=jnp.float32
    ) + lax.dot_general(
        pre[hidden:].astype(jnp.bfloat16), up_ref[...], down, preferred_element_type=jnp.float32
    )
    piece_ref[...] = piece.astype(jnp.bfloat16).reshape(piece_ref.shape)
    store = pltpu.make_async_copy(piece_ref, piece_hbm, sem)
    store.start()
    store.wait()


def combine_kernel(table_ref, rows_ref, tokens_ref):
    flat = rows_ref[...].reshape(table_ref.shape[0], tokens_ref.shape[1])
    total = lax.dot_general(
        table_ref[...], flat, (((0,), (0,)), ((), ())), preferred_element_type=jnp.float32
    )
    tokens_ref[...] = total.astype(jnp.bfloat16)


def added(first, second):
    return (first.astype(jnp.float32) + second.astype(jnp.float32)).astype(jnp.bfloat16)


def chip_kernel(replica_ref, mine_ref, theirs_ref, *out_refs):
    chips = len(out_refs)
    for distance, out_ref in enumerate(out_refs):
        chunk = ((replica_ref[0] >> 1) + distance) & (chips - 1)
        out_ref[...] = added(mine_ref[chunk], theirs_ref[chunk])


def add_kernel(got_ref, own_ref, sum_ref):
    sum_ref[...] = added(got_ref[...], own_ref[...])


def total_kernel(up_ring_ref, down_ring_ref, own_ref, gate_ref, up_ref, down_ref):
    hidden, width = gate_ref.shape
    total = up_ring_ref[...].astype(jnp.float32) + down_ring_ref[...].astype(jnp.float32)
    total = total + own_ref[...].astype(jnp.float32)
    for index, out_ref in enumerate((gate_ref, up_ref, down_ref)):
        rows = total[index * hidden : (index + 1) * hidden]
        out_ref[...] = rows[:, :width].astype(jnp.bfloat16)


def shards(tokens, cotangent, gates, route_ids, w_gate, w_up, w_down):
    device_count = lax.axis_size("expert")
    replicas = lax.axis_size("dp")
    pieces = device_count // EXPERTS
    token_count, feature_count = tokens.shape
    hidden = w_gate.shape[0]
    chips = replicas // 2
    width = feature_count // replicas
    lanes = -(-width // 128) * 128
    rows = device_count * CAP
    vmem = pl.BlockSpec(memory_space=pltpu.VMEM)
    smem = pl.BlockSpec(memory_space=pltpu.SMEM)
    hbm = pl.BlockSpec(memory_space=pltpu.HBM)
    in_hbm = functools.partial(pltpu.with_memory_space_constraint, memory_space=pltpu.HBM)
    send, table = pl.pallas_call(
        select_kernel,
        out_shape=(
            pltpu.HBM((EXPERTS, pieces, CAP, feature_count), jnp.bfloat16),
            jax.ShapeDtypeStruct((rows, token_count), jnp.bfloat16),
        ),
        in_specs=[hbm] * 4,
        out_specs=(hbm, vmem),
        scratch_shapes=[
            pltpu.VMEM((2, token_count), jnp.int32),
            pltpu.VMEM((2, token_count), jnp.bfloat16),
            pltpu.VMEM((token_count, feature_count), jnp.bfloat16),
            pltpu.VMEM((token_count, feature_count), jnp.bfloat16),
            pltpu.VMEM((2, EXPERTS, CAP, feature_count), jnp.bfloat16),
            pltpu.SemaphoreType.DMA((4,)),
            pltpu.SemaphoreType.DMA((pieces,)),
        ],
        compiler_params=pltpu.CompilerParams(vmem_limit_bytes=16 * 2**20),
    )(in_hbm(route_ids.T), in_hbm(gates.T), in_hbm(tokens), in_hbm(cotangent))
    arrived = lax.all_to_all(
        send.reshape(device_count, CAP, feature_count),
        "expert",
        split_axis=0,
        concat_axis=0,
        tiled=True,
    )
    ring = pieces // 2
    after = [(i, i // ring * ring + (i + 1) % ring) for i in range(device_count)]
    before = [(i, i // ring * ring + (i - 1) % ring) for i in range(device_count)]
    split = device_count * 9 // 16

    def part(start, size):
        return pl.pallas_call(
            functools.partial(part_kernel, start),
            out_shape=jax.ShapeDtypeStruct((size, CAP, feature_count), jnp.bfloat16),
            in_specs=[vmem],
            out_specs=vmem,
            compiler_params=pltpu.CompilerParams(vmem_limit_bytes=12 * 2**20),
        )(arrived)

    low, high = part(0, split), part(split, device_count - split)
    low = lax.ppermute(low, "expert", after)
    high = lax.ppermute(high, "expert", before)
    piece_at = lax.axis_index("expert").astype(jnp.int32).reshape(1)
    replica = lax.axis_index("dp").astype(jnp.int32).reshape(1)
    flat_lanes = feature_count + lanes // 2
    weight_shape = jax.ShapeDtypeStruct((hidden, feature_count), jnp.bfloat16)
    forward_shape = jax.ShapeDtypeStruct((2, hidden, rows), jnp.float32)
    back_shape = jax.ShapeDtypeStruct((hidden, rows), jnp.float32)
    first, up_here, down_here, forward, back = pl.pallas_call(
        first_kernel,
        out_shape=(
            jax.ShapeDtypeStruct((rows, flat_lanes), jnp.bfloat16),
            weight_shape,
            weight_shape,
            forward_shape,
            back_shape,
        ),
        in_specs=[smem, vmem, vmem, hbm, hbm],
        out_specs=(vmem,) * 5,
        scratch_shapes=[pltpu.SemaphoreType.DMA((2,))],
        compiler_params=pltpu.CompilerParams(vmem_limit_bytes=12 * 2**20),
        cost_estimate=pl.CostEstimate(
            flops=4 * hidden * rows * feature_count, bytes_accessed=8 * 2**20, transcendentals=0
        ),
    )(piece_at, arrived, w_gate, in_hbm(w_up), in_hbm(w_down))
    grads_shape = jax.ShapeDtypeStruct((chips, 3 * hidden, lanes), jnp.bfloat16)
    other, pre, activation, flat = pl.pallas_call(
        functools.partial(passes_kernel, width),
        out_shape=(
            grads_shape,
            jax.ShapeDtypeStruct((2 * hidden, rows), jnp.bfloat16),
            jax.ShapeDtypeStruct((hidden, rows), jnp.bfloat16),
            jax.ShapeDtypeStruct((2, rows, flat_lanes), jnp.bfloat16),
        ),
        in_specs=[smem, smem] + [vmem] * 8,
        out_specs=(vmem,) * 4,
        scratch_shapes=[
            pltpu.VMEM((2, hidden, rows), jnp.float32),
            pltpu.VMEM((hidden, rows), jnp.float32),
        ],
        compiler_params=pltpu.CompilerParams(vmem_limit_bytes=12 * 2**20),
    )(replica, piece_at, first, low, high, w_gate, up_here, down_here, forward, back)
    swap = [(i, i ^ 1) for i in range(replicas)]
    theirs = lax.ppermute(other, "dp", swap)
    mine = pl.pallas_call(
        functools.partial(own_kernel, width),
        out_shape=grads_shape,
        in_specs=[smem] + [vmem] * 3,
        out_specs=vmem,
        compiler_params=pltpu.CompilerParams(vmem_limit_bytes=12 * 2**20),
        cost_estimate=pl.CostEstimate(
            flops=6 * hidden * rows * feature_count, bytes_accessed=4 * 2**20, transcendentals=0
        ),
    )(replica, pre, activation, flat)
    chunk_shape = jax.ShapeDtypeStruct((3 * hidden, lanes), jnp.bfloat16)
    small = pltpu.CompilerParams(vmem_limit_bytes=12 * 2**20)
    chunks = pl.pallas_call(
        chip_kernel,
        out_shape=(chunk_shape,) * chips,
        in_specs=[smem, vmem, vmem],
        out_specs=(vmem,) * chips,
        compiler_params=small,
    )(replica, mine, theirs)
    add = pl.pallas_call(
        add_kernel,
        out_shape=chunk_shape,
        in_specs=[vmem, vmem],
        out_specs=vmem,
        compiler_params=small,
    )
    far = chips // 2
    chunks = list(chunks)
    piece_grad = pl.pallas_call(
        piece_kernel,
        out_shape=pltpu.HBM((device_count, CAP, feature_count), jnp.bfloat16),
        in_specs=[vmem] * 3,
        out_specs=hbm,
        scratch_shapes=[
            pltpu.VMEM((device_count, CAP, feature_count), jnp.bfloat16),
            pltpu.SemaphoreType.DMA(()),
        ],
        compiler_params=pltpu.CompilerParams(vmem_limit_bytes=12 * 2**20),
        cost_estimate=pl.CostEstimate(
            flops=4 * hidden * rows * feature_count, bytes_accessed=4 * 2**20, transcendentals=0
        ),
    )(pre, w_gate, up_here)
    chunks[far], piece_grad = lax.optimization_barrier((chunks[far], piece_grad))
    ahead = [(i, (i + 2) % replicas) for i in range(replicas)]
    back = [(i, (i - 2) % replicas) for i in range(replicas)]
    rising = lax.ppermute(chunks[far], "dp", ahead)
    falling = lax.ppermute(chunks[chips - far + 1], "dp", back)
    for distance in range(far - 1, 0, -1):
        rising = lax.ppermute(add(rising, chunks[distance]), "dp", ahead)
        if distance > 1:
            falling = lax.ppermute(add(falling, chunks[chips - distance + 1]), "dp", back)
    returned = lax.all_to_all(piece_grad, "expert", split_axis=0, concat_axis=0, tiled=True)
    grad_tokens = pl.pallas_call(
        combine_kernel,
        out_shape=jax.ShapeDtypeStruct((token_count, feature_count), jnp.bfloat16),
        in_specs=[vmem, vmem],
        out_specs=vmem,
        compiler_params=small,
        cost_estimate=pl.CostEstimate(
            flops=2 * rows * token_count * feature_count,
            bytes_accessed=2 * 2**20,
            transcendentals=0,
        ),
    )(table, returned)
    falling, grad_tokens = lax.optimization_barrier((falling, grad_tokens))
    owned = jax.ShapeDtypeStruct((hidden, width), jnp.bfloat16)
    grads = pl.pallas_call(
        total_kernel,
        out_shape=(owned,) * 3,
        in_specs=[vmem] * 3,
        out_specs=(vmem,) * 3,
        compiler_params=small,
    )(rising, falling, chunks[0])
    return (grad_tokens, *grads)


def solution(mesh):
    in_specs = (
        P(("expert", "dp"), None),
        P(("expert", "dp"), None),
        P(("expert", "dp"), None),
        P(("expert", "dp"), None),
        P("expert", None),
        P("expert", None),
        P("expert", None),
    )
    out_specs = (P(("expert", "dp"), None), P("expert", "dp"), P("expert", "dp"), P("expert", "dp"))
    return jax.shard_map(shards, mesh=mesh, in_specs=in_specs, out_specs=out_specs, check_vma=False)
```
